512 devices in a mesh: fsdp: 32 (over y, x), tensor: 16 (over z, core).
Axes of the slice: x: 4, y: 8, z: 8, core: 2. Of those that a mesh axis runs over, the one named last changes fastest.
Arguments:
- inputs: bfloat16 [8192, 8192], P('tensor', 'fsdp'), may hold values from -6 to 6
- grad_out: bfloat16 [8192, 8192], P('fsdp', 'tensor'), may hold values from -0.0625 to 0.0625
- filters: bfloat16 [512, 128], P('tensor'), may hold values from -0.5 to 0.5
- momentum: float32 [8192, 8192], P('fsdp', 'tensor'), may hold values from -6 to 6
- basis: float32 [8192, 256], P('tensor'), may hold values from -6 to 6
Outputs:
- update: bfloat16 [8192, 8192], P('fsdp', 'tensor')
- new_momentum: float32 [8192, 8192], P('fsdp', 'tensor')
- new_basis: float32 [8192, 256], P('tensor')
The draws below stay inside these ranges and needn't reach their ends.
All inputs are finite; a program needn't handle non-finite values.
Results may differ from the reference program's by a relative error of at most 0.0051.
Values may be sent and summed in bfloat16 or wider, within the bound.
A program may use at most 64 MiB of HBM per device.

```python
import math
import jax
import jax.numpy as jnp
from jax import lax

D = 8192
TAPS = 128
GROUP = 16
RANK = 256
TOKENS = 8192
FILTERS = 512


def draw_momentum(key, part):
    key = jax.random.fold_in(key, 11)
    return jax.random.truncated_normal(key, -6.0, 6.0, (D, D), jnp.float32)


def draw_basis(key, part):
    key = jax.random.fold_in(key, 23)
    return jax.random.truncated_normal(key, -6.0, 6.0, (D, RANK), jnp.float32)


def block_levels(rng, extent, pieces, least, high):
    factor_of, own = 1.0, jax.random.fold_in(rng, 6)
    for axis_at, parts in pieces:
        draws = jnp.exp(jax.random.uniform(jax.random.fold_in(own, axis_at), (parts,), jnp.float32, least / len(pieces), high / len(pieces)))
        factor_of = factor_of * jnp.repeat(draws, extent[axis_at] // parts).reshape([-1 if axis == axis_at else 1 for axis in range(len(extent))])
    return factor_of


def noise(key, dims, width, bound, pieces=(), kind=jnp.bfloat16):
    gain = block_levels(key, dims, pieces, -0.22, 0.18) if pieces else 1.0
    values = jax.random.normal(key, dims, jnp.float32) * width * gain
    return jnp.minimum(jnp.maximum(values, -bound), bound).astype(kind)


def setup_inputs(seed: int = 0) -> dict:
    key_of = jax.random.split(jax.random.key(seed), 6)
    return {
        "inputs": noise(key_of[0], (TOKENS, D), 1.0, 6.0, ((0, 16), (1, 32))),
        "grad_out": noise(key_of[1], (TOKENS, D), TOKENS ** -0.5, 0.0625, ((0, 32), (1, 16))),
        "filters": noise(key_of[2], (FILTERS, TAPS), TAPS ** -0.5, 0.5, ((0, 16),)),
        "momentum": draw_momentum(jax.random.fold_in(key_of[5], 71), 0),
        "basis": draw_basis(jax.random.fold_in(key_of[5], 71), 0),
    }


momentum_decay = 0.95
epsilon = 1e-06

def backward_conv(grad_out, filters):
    per_channel = jnp.repeat(filters.astype(jnp.float32), GROUP, axis=0)
    padded = jnp.concatenate([grad_out.astype(jnp.float32), jnp.zeros((TAPS, D), jnp.float32)], axis=0)

    def add_tap(position, running):
        window = lax.dynamic_slice_in_dim(padded, position, TOKENS, 0)
        weights = lax.dynamic_slice_in_dim(per_channel, position, 1, 1)
        return running + window * weights.reshape(1, D)
    total = lax.fori_loop(jnp.int32(0), jnp.int32(TAPS), add_tap, jnp.zeros((TOKENS, D), jnp.float32))
    return total.astype(jnp.bfloat16)

def reference(inputs, grad_out, filters, momentum, basis):
    highest = lax.Precision.HIGHEST
    grad_mixed = backward_conv(grad_out, filters)
    gradient = lax.dot_general(inputs.astype(jnp.float32), grad_mixed.astype(jnp.float32), (((0,), (0,)), ((), ())), preferred_element_type=jnp.float32)
    blended = momentum + gradient
    sketch = jnp.dot(blended, basis, precision=highest)
    gram_matrix = jnp.dot(sketch.T, sketch, precision=highest)
    factor = jnp.linalg.cholesky(gram_matrix)
    orthonormal = jax.scipy.linalg.solve_triangular(factor, sketch.T, lower=True).T
    projected = jnp.dot(blended.T, orthonormal, precision=highest)
    squares = lax.optimization_barrier(jnp.sum(projected * projected, axis=0))
    new_basis = projected / jnp.sqrt(squares / D + epsilon)
    new_momentum = blended - (1.0 - momentum_decay) * jnp.dot(orthonormal, projected.T, precision=highest)
    update = (math.sqrt(D / RANK) * jnp.dot(orthonormal, new_basis.T, precision=highest)).astype(jnp.bfloat16)
    return (update, new_momentum, new_basis)
```

```python
import functools
import math

import jax
import jax.numpy as jnp
from jax import lax
from jax.experimental import pallas as pl
from jax.experimental.pallas import tpu as pltpu
from jax.sharding import PartitionSpec as P

D = 8192
GROUP = 16
RANK = 256
TAPS = 128
HALF = 128

momentum_decay = 0.95
epsilon = 1e-06

MESH = pl.DeviceIdType.MESH
HIGHEST = lax.Precision.HIGHEST
VMEM = pl.BlockSpec(memory_space=pltpu.VMEM)


class Place:
    def __init__(self, sizes):
        self.X, self.Y, self.Z = sizes
        self.F, self.T = self.X * self.Y, self.Z * 2
        self.f, self.t = lax.axis_index("fsdp"), lax.axis_index("tensor")
        self.y, self.x = self.f // self.X, lax.rem(self.f, self.X)
        self.z, self.c = self.t // 2, lax.rem(self.t, 2)

    def wrap(self, value, n):
        return lax.rem(value + 2 * n, n)

    def plane(self, dy, dx):
        return (self.wrap(self.y + dy, self.Y) * self.X + self.wrap(self.x + dx, self.X), self.t)

    def along_z(self, dz):
        return (self.f, self.wrap(self.z + dz, self.Z) * 2 + self.c)

    def sibling(self):
        return (self.f, self.z * 2 + 1 - self.c)

    def fsdp(self, d):
        return (self.wrap(self.f + d, self.F), self.t)

    def tensor(self, d):
        return (self.f, self.wrap(self.t + d, self.T))


def greet(peers):
    barrier = pltpu.get_barrier_semaphore()
    for peer in peers:
        pl.semaphore_signal(barrier, inc=1, device_id=peer, device_id_type=MESH)


def all_greeted(peers):
    pl.semaphore_wait(pltpu.get_barrier_semaphore(), len(peers))


def remote(src, dst, send, recv, peer):
    return pltpu.make_async_remote_copy(
        src_ref=src, dst_ref=dst, send_sem=send, recv_sem=recv, device_id=peer, device_id_type=MESH
    )


def ring(n, axis, rows, tell, first):
    lo, count = rows
    half = n // 2
    pieces = [(0, rows, first)]
    for sign in (1, -1):
        before = first
        for step in range(1, half + 1):
            part = rows
            if step == half:
                part = (lo, count // 2) if sign > 0 else (lo + count // 2, count // 2)
            before = tell(axis, sign, sign * (step - 1), part, before)
            pieces.append((sign * step, part, before))
    return pieces


def plan(sizes):
    X, Y, Z = sizes
    messages = []

    def teller(part, fixed):
        def tell(axis, sign, offset, rows, needs):
            where = dict(fixed)
            where[axis] = offset
            messages.append(dict(part=part, axis=axis, sign=sign, at=where, rows=rows, needs=needs))
            return len(messages) - 1

        return tell

    for ox, rows, needs in ring(X, "x", (0, HALF), teller("A", {"y": 0}), "A"):
        ring(Y, "y", rows, teller("A", {"x": ox}), needs)
    for oy, rows, needs in ring(Y, "y", (0, HALF), teller("B", {"x": 0}), "B"):
        ring(X, "x", rows, teller("B", {"y": oy}), needs)
    for oz, rows, needs in ring(Z, "z", (0, 256), teller("I", {}), "I"):
        teller("I", {"z": oz})("c", 1, 0, rows, needs)
    ready = {"I": 0.5, "B": 1.5, "A": 5.0}
    free, arrival = {}, {}
    waiting = list(range(len(messages)))
    while waiting:
        when = {m: ready[messages[m]["needs"]] for m in waiting if messages[m]["needs"] in ready}
        best = min(when, key=lambda m: (max(when[m], free.get((messages[m]["axis"], messages[m]["sign"]), 0)), when[m], m))
        message = messages[best]
        link = (message["axis"], message["sign"])
        start = max(when[best], free.get(link, 0.0))
        length = message["rows"][1] * 1024 * (2 / 1e5 if link[0] != "c" else 1 / 4e5)
        free[link] = start + length
        ready[best] = arrival[best] = start + length + 1.8
        message["starts"] = start
        waiting.remove(best)
    order = sorted(arrival, key=lambda m: arrival[m])
    return messages, order, arrival


def strided_taps(filters, toeplitz_ref):
    count = filters.shape[0]
    wide = jnp.concatenate([filters, jnp.zeros_like(filters)], axis=1)
    for g in range(count):
        rows = jnp.broadcast_to(wide[g : g + 1, :], (TAPS, 2 * TAPS))
        rolled = pltpu.roll(rows, 0, 1, stride=1, stride_axis=0)
        toeplitz_ref[g * TAPS : (g + 1) * TAPS, :] = rolled.astype(jnp.bfloat16)


def convolve(toeplitz_ref, window):
    channels = window.shape[1]
    group = lax.broadcasted_iota(jnp.int32, (TAPS, 128), 1) // GROUP
    each = 128 // GROUP
    columns = []
    for q in range(channels // 128):
        product = jnp.dot(
            toeplitz_ref[q * each * TAPS : (q + 1) * each * TAPS, :],
            window[:, q * 128 : (q + 1) * 128],
            preferred_element_type=jnp.float32,
        )
        total = product[:TAPS]
        for i in range(1, each):
            total = jnp.where(group == i, product[i * TAPS : (i + 1) * TAPS], total)
        columns.append(total)
    return jnp.concatenate(columns, axis=1).astype(jnp.bfloat16)


def gather_kernel(
    sizes, inputs_ref, grad_ref, filters_ref, momentum_ref, basis_ref, blended_ref, sketch_ref,
    halo, toeplitz, first, second, features, halo_sem, send_sem, recv_sem,
):
    me = Place(sizes)
    peers = [me.plane(0, 1), me.plane(0, -1), me.plane(1, 0), me.plane(-1, 0)]
    peers += [me.along_z(1), me.along_z(-1), me.sibling(), me.fsdp(1), me.fsdp(-1)]
    greet(peers)
    messages, order, _ = plan(sizes)
    strided_taps(filters_ref[...].astype(jnp.float32), toeplitz)
    features[me.t] = jnp.transpose(inputs_ref[...].astype(jnp.float32)).astype(jnp.bfloat16)
    all_greeted(peers)

    def copy_of(m, arriving):
        message = messages[m]
        sign = message["sign"]
        shift = sign if arriving else 0
        at, axis = dict(message["at"]), message["axis"]
        rows = pl.ds(*message["rows"])
        if axis in at:
            at[axis] += shift
        if message["part"] == "I":
            core = me.c
            if axis == "c" and arriving:
                core = 1 - me.c
            block = features.at[me.wrap(me.z - at["z"], me.Z) * 2 + core, rows]
            peer = me.sibling() if axis == "c" else me.along_z(sign)
        else:
            y, x = me.wrap(me.y - at["y"], me.Y), me.wrap(me.x - at["x"], me.X)
            block = second.at[y, x, rows] if message["part"] == "A" else first.at[x, y, rows]
            peer = me.plane(0, sign) if axis == "x" else me.plane(sign, 0)
        return remote(block, block, send_sem.at[m], recv_sem.at[m], peer)

    def start_after(event):
        for m in sorted((m for m in range(len(messages)) if messages[m]["needs"] == event), key=lambda m: messages[m]["starts"]):
            copy_of(m, False).start()

    halo_copy = remote(grad_ref.at[pl.ds(0, TAPS)], halo, halo_sem.at[0], halo_sem.at[1], me.fsdp(-1))
    halo_copy.start()
    start_after("I")
    first[me.x, me.y] = convolve(toeplitz, grad_ref[...])
    start_after("B")
    halo_copy.wait_recv()
    tail = jnp.where(me.f == me.F - 1, jnp.zeros_like(halo[...]), halo[...])
    second[me.y, me.x] = convolve(toeplitz, jnp.concatenate([grad_ref[TAPS:, :], tail], axis=0))
    start_after("A")
    for m in order:
        copy_of(m, True).wait_recv()
        start_after(m)
    halo_copy.wait_send()
    for m in order:
        copy_of(m, False).wait_send()

    blended_ref[...] = momentum_ref[...]

    def add(f, carry):
        y, x = f // me.X, lax.rem(f, me.X)
        rows = jnp.concatenate([first[x, y], second[y, x]], axis=0)
        columns = pl.ds(pl.multiple_of(lax.rem(f, 2) * 2 * TAPS, 2 * TAPS), 2 * TAPS)
        blended_ref[...] += jnp.dot(features[f // 2, :, columns], rows, preferred_element_type=jnp.float32)
        return carry

    lax.fori_loop(0, me.F, add, 0)
    sketch_ref[...] = jnp.dot(blended_ref[...], basis_ref[...], precision=HIGHEST, preferred_element_type=jnp.float32)


def rows_dot(left, right):
    return lax.dot_general(
        left, right, (((0,), (0,)), ((), ())), precision=HIGHEST, preferred_element_type=jnp.float32
    )


def dot_t(left, right):
    return lax.dot_general(
        left, right, (((1,), (1,)), ((), ())), precision=HIGHEST, preferred_element_type=jnp.float32
    )


def dot(left, right):
    return jnp.dot(left, right, precision=HIGHEST, preferred_element_type=jnp.float32)


def sum_kernel(
    sizes, partial_ref, blended_ref, sketch_ref, gram_ref, right_ref,
    half_in, half_sum, z_in, gram_part, right_part, gram_in, right_in,
    core_sem, z_send, z_recv, f_send, f_recv,
):
    me = Place(sizes)
    peers = [me.sibling()] + [me.along_z(d) for d in range(1, me.Z)] + [me.fsdp(d) for d in range(1, me.F)]
    greet(peers)
    all_greeted(peers)
    half = partial_ref.shape[0] // 2
    mine = pl.ds(pl.multiple_of(me.c * half, 8), half)
    other = pl.ds(pl.multiple_of((1 - me.c) * half, 8), half)
    swap = remote(partial_ref.at[other], half_in, core_sem.at[0], core_sem.at[1], me.sibling())
    swap.start()
    swap.wait()
    half_sum[...] = partial_ref[mine, :] + half_in[...]
    piece = half // me.Z

    def z_rows(z, base):
        return pl.ds(pl.multiple_of(base + z * piece, 8), piece)

    out = []
    for d in range(1, me.Z):
        out.append(remote(half_sum.at[z_rows(me.wrap(me.z + d, me.Z), 0)], z_in.at[d], z_send.at[0, d], z_recv.at[0, d], me.along_z(d)))
        out[-1].start()
    total = half_sum[z_rows(me.z, 0), :]
    for d in range(1, me.Z):
        out[d - 1].wait_recv()
        total = total + z_in[d]
    held = z_rows(me.z, me.c * half)
    sketch_ref[held, :] = total
    for d in range(1, me.Z):
        out.append(remote(sketch_ref.at[held], sketch_ref.at[held], z_send.at[1, d], z_recv.at[1, d], me.along_z(d)))
        out[-1].start()
    for d in range(1, me.Z):
        there = sketch_ref.at[z_rows(me.wrap(me.z - d, me.Z), me.c * half)]
        remote(there, there, z_send.at[1, d], z_recv.at[1, d], me.along_z(d)).wait_recv()
    swap = remote(sketch_ref.at[mine], sketch_ref.at[mine], core_sem.at[2], core_sem.at[3], me.sibling())
    swap.start()
    swap.wait_send()
    remote(sketch_ref.at[other], sketch_ref.at[other], core_sem.at[2], core_sem.at[3], me.sibling()).wait_recv()
    sketch = sketch_ref[...]

    def scatter(kind, part, into):
        rows = part.shape[0] // me.F
        for d in range(1, me.F):
            there = pl.ds(pl.multiple_of(me.wrap(me.f + d, me.F) * rows, 8), rows)
            out.append(remote(part.at[there], into.at[d], f_send.at[kind, d], f_recv.at[kind, d], me.fsdp(d)))
            out[-1].start()

    def collect(kind, part, into, result):
        rows = part.shape[0] // me.F
        here = pl.ds(pl.multiple_of(me.f * rows, 8), rows)
        total = part[here, :]
        for d in range(1, me.F):
            remote(into.at[d], into.at[d], f_send.at[kind, d], f_recv.at[kind, d], me.fsdp(d)).wait_recv()
            total = total + into[d]
        result[here, :] = total
        for d in range(1, me.F):
            out.append(remote(result.at[here], result.at[here], f_send.at[kind + 1, d], f_recv.at[kind + 1, d], me.fsdp(d)))
            out[-1].start()

    def arrive(kind, result):
        rows = result.shape[0] // me.F
        for d in range(1, me.F):
            there = result.at[pl.ds(pl.multiple_of(me.wrap(me.f - d, me.F) * rows, 8), rows)]
            remote(there, there, f_send.at[kind, d], f_recv.at[kind, d], me.fsdp(d)).wait_recv()

    gram_part[...] = rows_dot(sketch, sketch)
    scatter(0, gram_part, gram_in)
    right_part[...] = rows_dot(blended_ref[...], sketch)
    scatter(2, right_part, right_in)
    collect(0, gram_part, gram_in, gram_ref)
    collect(2, right_part, right_in, right_ref)
    arrive(1, gram_ref)
    arrive(3, right_ref)
    for copy in out:
        copy.wait_send()


def inverse_factor(rows):
    shape = (8, 128)
    rows = list(rows)
    lane = lax.broadcasted_iota(jnp.int32, shape, 1)
    sub = lax.broadcasted_iota(jnp.int32, shape, 0)

    def column(value, k):
        return jnp.broadcast_to(value[:, k : k + 1], shape)

    def row(value, k):
        return jnp.broadcast_to(value[k : k + 1, :], shape)

    for b in range(len(rows)):
        base = 8 * b
        pivot = rows[b]
        columns = [column(pivot, base + j) for j in range(8)]
        inside = (lane >= base) & (lane < base + 8)
        pivot = jnp.where(inside, jnp.where(lane - base == sub, 1.0, 0.0), pivot)
        scale = jnp.zeros(shape, jnp.float32)
        inverses, uppers, crossed = [], [], {}
        for j in range(8):
            diagonal = row(columns[j], j)
            inverse = 1.0 / diagonal
            lower = jnp.where(sub > j, columns[j] * inverse, 0.0)
            scale = jnp.where(sub == j, lax.rsqrt(diagonal), scale)
            for k in range(j + 1, 8):
                crossed[j, k] = row(columns[k], j)
                columns[k] = columns[k] - lower * crossed[j, k]
            upper = row(pivot, j)
            pivot = pivot - lower * upper
            inverses.append(inverse)
            uppers.append(upper)
        rows[b] = jnp.where(lane < base + 8, pivot * scale, 0.0)
        for i in range(b + 1, len(rows)):
            below = rows[i]
            columns = [column(below, base + j) for j in range(8)]
            below = jnp.where(inside, 0.0, below)
            for j in range(8):
                lower = columns[j] * inverses[j]
                for k in range(j + 1, 8):
                    columns[k] = columns[k] - lower * crossed[j, k]
                below = below - lower * uppers[j]
            rows[i] = below
    return rows


def by_eight(block):
    return [block[8 * i : 8 * i + 8, :] for i in range(block.shape[0] // 8)]


def factor_kernel(gram_ref, inverse_ref):
    h = gram_ref.shape[0] // 2
    top = jnp.concatenate(inverse_factor(by_eight(gram_ref[:h, :h])), axis=0)
    lower = dot_t(gram_ref[h:, :h], top)
    rest = gram_ref[h:, h:] - dot_t(lower, lower)
    bottom = jnp.concatenate(inverse_factor(by_eight(rest)), axis=0)
    inverse_ref[:h, :h] = top
    inverse_ref[:h, h:] = jnp.zeros((h, h), jnp.float32)
    inverse_ref[h:, :h] = -dot(bottom, dot(lower, top))
    inverse_ref[h:, h:] = bottom


def finish_kernel(
    sizes, sketch_ref, right_ref, inverse_ref, blended_ref, update_ref, momentum_ref, basis_ref, squares, send_sem, recv_sem
):
    me = Place(sizes)
    peers = [me.tensor(d) for d in range(1, me.T)]
    greet(peers)
    inverse = inverse_ref[...]
    projected = dot_t(right_ref[...], inverse)
    squares[0] = jnp.sum(projected * projected, axis=0, keepdims=True)
    all_greeted(peers)
    out = []
    for d in range(1, me.T):
        out.append(remote(squares.at[0], squares.at[d], send_sem.at[d], recv_sem.at[d], me.tensor(d)))
        out[-1].start()
    orthonormal = dot_t(sketch_ref[...], inverse)
    momentum_ref[...] = blended_ref[...] - (1.0 - momentum_decay) * dot_t(orthonormal, projected)
    total = squares[0]
    for d in range(1, me.T):
        out[d - 1].wait_recv()
        total = total + squares[d]
    new_basis = projected / jnp.sqrt(total / D + epsilon)
    basis_ref[...] = new_basis
    update_ref[...] = (math.sqrt(D / RANK) * dot_t(orthonormal, new_basis)).astype(jnp.bfloat16)
    for copy in out:
        copy.wait_send()


def call(kernel, name, outs, scratch, collective, *args, flops=0):
    params = dict(vmem_limit_bytes=48 << 20)
    if collective is not None:
        params.update(collective_id=collective, has_side_effects=True)
    return pl.pallas_call(
        kernel,
        name=name,
        out_shape=[jax.ShapeDtypeStruct(shape, dtype) for shape, dtype in outs],
        in_specs=[VMEM] * len(args),
        out_specs=[VMEM] * len(outs),
        scratch_shapes=scratch,
        compiler_params=pltpu.CompilerParams(**params),
        cost_estimate=pl.CostEstimate(flops=flops, bytes_accessed=4 << 20, transcendentals=0),
    )(*args)


def shards(sizes, inputs, grad_out, filters, momentum, basis):
    X, Y, Z = sizes
    F, T = X * Y, 2 * Z
    dma = pltpu.SemaphoreType.DMA
    f32, bf16 = jnp.float32, jnp.bfloat16
    tokens, channels = grad_out.shape
    width = inputs.shape[1]
    messages, _, _ = plan(sizes)
    blended, partial = call(
        functools.partial(gather_kernel, sizes), "gather",
        [((width, channels), f32), ((width, RANK), f32)],
        [
            pltpu.VMEM((TAPS, channels), bf16),
            pltpu.VMEM((filters.shape[0] * TAPS, 2 * TAPS), bf16),
            pltpu.VMEM((X, Y, HALF, channels), bf16),
            pltpu.VMEM((Y, X, HALF, channels), bf16),
            pltpu.VMEM((T, width, inputs.shape[0]), bf16),
            dma((2,)), dma((len(messages),)), dma((len(messages),)),
        ],
        1, inputs, grad_out, filters, momentum, basis, flops=3 * 10**9,
    )
    half = width // 2
    sketch, gram, right = call(
        functools.partial(sum_kernel, sizes), "sums",
        [((width, RANK), f32), ((RANK, RANK), f32), ((channels, RANK), f32)],
        [
            pltpu.VMEM((half, RANK), f32), pltpu.VMEM((half, RANK), f32),
            pltpu.VMEM((Z, half // Z, RANK), f32),
            pltpu.VMEM((RANK, RANK), f32), pltpu.VMEM((channels, RANK), f32),
            pltpu.VMEM((F, RANK // F, RANK), f32), pltpu.VMEM((F, channels // F, RANK), f32),
            dma((4,)), dma((2, Z)), dma((2, Z)), dma((4, F)), dma((4, F)),
        ],
        2, partial, blended, flops=10**9,
    )
    (inverse,) = call(factor_kernel, "factor", [((RANK, RANK), f32)], [], None, gram, flops=10**9)
    return tuple(call(
        functools.partial(finish_kernel, sizes), "finish",
        [((width, channels), bf16), ((width, channels), f32), ((channels, RANK), f32)],
        [pltpu.VMEM((T, 1, RANK), f32), dma((T,)), dma((T,))],
        3, sketch, right, inverse, blended, flops=10**9,
    ))


def solution(mesh):
    fsdp, tensor = mesh.shape["fsdp"], mesh.shape["tensor"]
    X = 4 if fsdp == 32 else 2
    placed = (
        P("tensor", "fsdp"),
        P("fsdp", "tensor"),
        P("tensor", None),
        P("fsdp", "tensor"),
        P("tensor", None),
    )
    return jax.shard_map(
        functools.partial(shards, (X, fsdp // X, tensor // 2)),
        mesh=mesh,
        in_specs=placed,
        out_specs=(P("fsdp", "tensor"), P("fsdp", "tensor"), P("tensor", None)),
        check_vma=False,
    )
```

```python
import functools
import math

import jax
import jax.numpy as jnp
from jax import lax
from jax.experimental import pallas as pl
from jax.experimental.pallas import tpu as pltpu
from jax.sharding import PartitionSpec as P

D = 8192
GROUP = 16
RANK = 256
TAPS = 128
HALF = 128

WHEN = (7.5, 14.0, 29.5, 34.0, 40.0, 46.0, 47.5, 57.0)

momentum_decay = 0.95
epsilon = 1e-06

MESH = pl.DeviceIdType.MESH
HIGHEST = lax.Precision.HIGHEST
VMEM = pl.BlockSpec(memory_space=pltpu.VMEM)
ANY = pl.BlockSpec(memory_space=pl.ANY)


class Place:
    def __init__(self, sizes):
        self.X, self.Y, self.Z = sizes
        self.F, self.T = self.X * self.Y, self.Z * 2
        self.f, self.t = lax.axis_index("fsdp"), lax.axis_index("tensor")
        self.y, self.x = self.f // self.X, lax.rem(self.f, self.X)
        self.z, self.c = self.t // 2, lax.rem(self.t, 2)

    def wrap(self, value, n):
        return lax.rem(value + 2 * n, n)

    def plane(self, dy, dx):
        return (self.wrap(self.y + dy, self.Y) * self.X + self.wrap(self.x + dx, self.X), self.t)

    def along_z(self, dz):
        return (self.f, self.wrap(self.z + dz, self.Z) * 2 + self.c)

    def sibling(self):
        return (self.f, self.z * 2 + 1 - self.c)

    def fsdp(self, d):
        return (self.wrap(self.f + d, self.F), self.t)

    def tensor(self, d):
        return (self.f, self.wrap(self.t + d, self.T))


def greet(peers):
    barrier = pltpu.get_barrier_semaphore()
    for peer in peers:
        pl.semaphore_signal(barrier, inc=1, device_id=peer, device_id_type=MESH)


def all_greeted(peers):
    pl.semaphore_wait(pltpu.get_barrier_semaphore(), len(peers))


def remote(src, dst, send, recv, peer):
    return pltpu.make_async_remote_copy(
        src_ref=src, dst_ref=dst, send_sem=send, recv_sem=recv, device_id=peer, device_id_type=MESH
    )


def ring(n, axis, rows, tell, first):
    lo, count = rows
    half = n // 2
    pieces = [(0, rows, first)]
    for sign in (1, -1):
        before = first
        for step in range(1, half + 1):
            part = rows
            if step == half:
                part = (lo, count // 2) if sign > 0 else (lo + count // 2, count // 2)
            before = tell(axis, sign, sign * (step - 1), part, before)
            pieces.append((sign * step, part, before))
    return pieces


def plan(sizes):
    X, Y, Z = sizes
    messages = []

    def teller(part, fixed):
        def tell(axis, sign, offset, rows, needs):
            where = dict(fixed)
            where[axis] = offset
            messages.append(dict(part=part, axis=axis, sign=sign, at=where, rows=rows, needs=needs))
            return len(messages) - 1

        return tell

    for ox, rows, needs in ring(X, "x", (0, HALF), teller("A", {"y": 0}), "A"):
        ring(Y, "y", rows, teller("A", {"x": ox}), needs)
    for oy, rows, needs in ring(Y, "y", (0, HALF), teller("B", {"x": 0}), "B"):
        ring(X, "x", rows, teller("B", {"y": oy}), needs)
    for oz, rows, needs in ring(Z, "z", (0, 256), teller("I", {}), "I"):
        teller("I", {"z": oz})("c", 1, 0, rows, needs)
    ready = {"I": 0.3, "B": 2.5, "A": 5.5}
    free, arrival = {}, {}
    waiting = list(range(len(messages)))
    while waiting:
        when = {m: ready[messages[m]["needs"]] for m in waiting if messages[m]["needs"] in ready}
        best = min(when, key=lambda m: (max(when[m], free.get((messages[m]["axis"], messages[m]["sign"]), 0)), when[m], m))
        message = messages[best]
        link = (message["axis"], message["sign"])
        start = max(when[best], free.get(link, 0.0))
        length = message["rows"][1] * 1024 * (2 / 1e5 if link[0] != "c" else 1 / 4e5)
        free[link] = start + length
        ready[best] = arrival[best] = start + length + 1.8
        message["starts"] = start
        waiting.remove(best)
    order = sorted(arrival, key=lambda m: arrival[m])
    return messages, order, arrival


def strided_taps(filters, toeplitz_ref):
    shape = (TAPS, TAPS)
    upper = lax.broadcasted_iota(jnp.int32, shape, 1) >= lax.broadcasted_iota(jnp.int32, shape, 0)
    for g in range(filters.shape[0]):
        rolled = pltpu.roll(jnp.broadcast_to(filters[g : g + 1, :], shape), 0, 1, stride=1, stride_axis=0)
        rows = pl.ds(g * TAPS, TAPS)
        toeplitz_ref[rows, :TAPS] = jnp.where(upper, rolled, 0.0).astype(jnp.bfloat16)
        toeplitz_ref[rows, TAPS:] = jnp.where(upper, 0.0, rolled).astype(jnp.bfloat16)


def convolve(toeplitz_ref, window):
    channels = window.shape[1]
    group = lax.broadcasted_iota(jnp.int32, (TAPS, 128), 1) // GROUP
    each = 128 // GROUP
    columns = []
    for q in range(channels // 128):
        product = jnp.dot(
            toeplitz_ref[q * each * TAPS : (q + 1) * each * TAPS, :],
            window[:, q * 128 : (q + 1) * 128],
            preferred_element_type=jnp.float32,
        )
        total = product[:TAPS]
        for i in range(1, each):
            total = jnp.where(group == i, product[i * TAPS : (i + 1) * TAPS], total)
        columns.append(total)
    return jnp.concatenate(columns, axis=1).astype(jnp.bfloat16)


def rows_dot(left, right):
    return lax.dot_general(
        left, right, (((0,), (0,)), ((), ())), precision=HIGHEST, preferred_element_type=jnp.float32
    )


def dot_t(left, right):
    return lax.dot_general(
        left, right, (((1,), (1,)), ((), ())), precision=HIGHEST, preferred_element_type=jnp.float32
    )


def dot(left, right):
    return jnp.dot(left, right, precision=HIGHEST, preferred_element_type=jnp.float32)


def inverse_factor(rows):
    shape = (8, 128)
    rows = list(rows)
    lane = lax.broadcasted_iota(jnp.int32, shape, 1)
    sub = lax.broadcasted_iota(jnp.int32, shape, 0)

    def column(value, k):
        return jnp.broadcast_to(value[:, k : k + 1], shape)

    def row(value, k):
        return jnp.broadcast_to(value[k : k + 1, :], shape)

    for b in range(len(rows)):
        base = 8 * b
        pivot = rows[b]
        columns = [column(pivot, base + j) for j in range(8)]
        inside = (lane >= base) & (lane < base + 8)
        pivot = jnp.where(inside, jnp.where(lane - base == sub, 1.0, 0.0), pivot)
        scale = jnp.zeros(shape, jnp.float32)
        inverses, uppers, crossed = [], [], {}
        for j in range(8):
            diagonal = row(columns[j], j)
            inverse = 1.0 / diagonal
            lower = jnp.where(sub > j, columns[j] * inverse, 0.0)
            scale = jnp.where(sub == j, lax.rsqrt(diagonal), scale)
            for k in range(j + 1, 8):
                crossed[j, k] = row(columns[k], j)
                columns[k] = columns[k] - lower * crossed[j, k]
            upper = row(pivot, j)
            pivot = pivot - lower * upper
            inverses.append(inverse)
            uppers.append(upper)
        rows[b] = jnp.where(lane < base + 8, pivot * scale, 0.0)
        for i in range(b + 1, len(rows)):
            below = rows[i]
            columns = [column(below, base + j) for j in range(8)]
            below = jnp.where(inside, 0.0, below)
            for j in range(8):
                lower = columns[j] * inverses[j]
                for k in range(j + 1, 8):
                    columns[k] = columns[k] - lower * crossed[j, k]
                below = below - lower * uppers[j]
            rows[i] = below
    return rows


def by_eight(block):
    return [block[8 * i : 8 * i + 8, :] for i in range(block.shape[0] // 8)]


def in_three(value):
    high = value.astype(jnp.bfloat16)
    rest = value - high.astype(jnp.float32)
    middle = rest.astype(jnp.bfloat16)
    low = (rest - middle.astype(jnp.float32)).astype(jnp.bfloat16)
    return jnp.concatenate([high, middle, low], axis=1)


def three_dot(left, right):
    n = right.shape[1] // 3
    product = jnp.dot(left, right, preferred_element_type=jnp.float32)
    return product[:, :n] + (product[:, n : 2 * n] + product[:, 2 * n :])


def main_kernel(
    sizes, inputs_hbm, grad_hbm, filters_hbm, momentum_hbm, basis_hbm,
    orthonormal_ref, projected_ref, momentum_ref, scale_ref,
    inputs_ref, grad_ref, filters_ref, basis_ref, blended_ref,
    halo, toeplitz, first, second, features,
    mixed, mixed_in, mixed_half, mixed_z, mixed_all,
    partial, half_in, half_sum, z_in, sketch_ref,
    gram_part, gram_in, gram_all, right_part, right_in, right_ref, squares,
    load_sem, halo_sem, send_sem, recv_sem, core_sem, z_send, z_recv, f_send, f_recv, t_send, t_recv,
):
    me = Place(sizes)
    loads = [
        pltpu.make_async_copy(there, here, load_sem.at[i])
        for i, (there, here) in enumerate([
            (inputs_hbm, inputs_ref), (grad_hbm, grad_ref), (filters_hbm, filters_ref),
            (basis_hbm, basis_ref), (momentum_hbm, blended_ref),
        ])
    ]
    for load in loads:
        load.start()
    peers = [me.fsdp(d) for d in range(1, me.F)] + [me.tensor(d) for d in range(1, me.T)]
    greet(peers)
    messages, order, arrival = plan(sizes)
    loads[0].wait()
    features[me.t] = jnp.transpose(inputs_ref[...].astype(jnp.float32)).astype(jnp.bfloat16)
    loads[1].wait()
    all_greeted(peers)

    def copy_of(m, arriving):
        message = messages[m]
        sign = message["sign"]
        shift = sign if arriving else 0
        at, axis = dict(message["at"]), message["axis"]
        rows = pl.ds(*message["rows"])
        if axis in at:
            at[axis] += shift
        if message["part"] == "I":
            core = me.c
            if axis == "c" and arriving:
                core = 1 - me.c
            block = features.at[me.wrap(me.z - at["z"], me.Z) * 2 + core, rows]
            peer = me.sibling() if axis == "c" else me.along_z(sign)
        else:
            y, x = me.wrap(me.y - at["y"], me.Y), me.wrap(me.x - at["x"], me.X)
            block = second.at[y, x, rows] if message["part"] == "A" else first.at[x, y, rows]
            peer = me.plane(0, sign) if axis == "x" else me.plane(sign, 0)
        return remote(block, block, send_sem.at[m], recv_sem.at[m], peer)

    def start_after(event):
        for m in sorted((m for m in range(len(messages)) if messages[m]["needs"] == event), key=lambda m: messages[m]["starts"]):
            copy_of(m, False).start()

    def add(oy, ox):
        y, x = me.wrap(me.y - oy, me.Y), me.wrap(me.x - ox, me.X)
        f = y * me.X + x
        rows = jnp.concatenate([first[x, y], second[y, x]], axis=0)
        columns = pl.ds(pl.multiple_of(lax.rem(f, 2) * 2 * TAPS, 2 * TAPS), 2 * TAPS)
        blended_ref[...] += jnp.dot(features[f // 2, :, columns], rows, preferred_element_type=jnp.float32)

    have = {(part, 0, 0): HALF for part in "AB"}
    ready, pending = [(0, 0)], list(order)
    adding = []

    def features_here():
        return not any(messages[m]["part"] == "I" for m in pending)

    def pump(until):
        while pending and arrival[pending[0]] <= until:
            m = pending.pop(0)
            copy_of(m, True).wait_recv()
            start_after(m)
            message = messages[m]
            if message["part"] != "I":
                at = dict(message["at"])
                at[message["axis"]] += message["sign"]
                place = (at["y"] % me.Y, at["x"] % me.X)
                have[(message["part"],) + place] = have.get((message["part"],) + place, 0) + message["rows"][1]
                if have.get(("A",) + place) == HALF and have.get(("B",) + place) == HALF:
                    ready.append(place)
            if adding and features_here() and ready:
                add(*ready.pop(0))

    out = []

    def send(*args):
        out.append(remote(*args))
        out[-1].start()

    def drain():
        for copy in out:
            copy.wait_send()
        out.clear()

    send(grad_ref.at[pl.ds(0, TAPS)], halo, halo_sem.at[0], halo_sem.at[1], me.fsdp(-1))
    start_after("I")
    loads[2].wait()
    strided_taps(filters_ref[...].astype(jnp.float32), toeplitz)
    first[me.x, me.y] = convolve(toeplitz, grad_ref[...])
    start_after("B")
    loads[3].wait()
    basis_terms = in_three(basis_ref[...])
    mixed[:TAPS, :] = three_dot(first[me.x, me.y], basis_terms)
    out[0].wait_recv()
    tail = jnp.where(me.f == me.F - 1, jnp.zeros_like(halo[...]), halo[...])
    second[me.y, me.x] = convolve(toeplitz, jnp.concatenate([grad_ref[TAPS:, :], tail], axis=0))
    start_after("A")
    mixed[TAPS:, :] = three_dot(second[me.y, me.x], basis_terms)

    half = TAPS
    piece = half // me.Z
    mine = pl.ds(pl.multiple_of(me.c * half, 8), half)
    other = pl.ds(pl.multiple_of((1 - me.c) * half, 8), half)

    def z_rows(z, base):
        return pl.ds(pl.multiple_of(base + z * piece, 8), piece)

    def core_swap(kind, there, here):
        send(there, here, core_sem.at[kind, 0], core_sem.at[kind, 1], me.sibling())

    def core_here(kind, here):
        remote(here, here, core_sem.at[kind, 0], core_sem.at[kind, 1], me.sibling()).wait_recv()

    def z_scatter(kind, source, into):
        for d in range(1, me.Z):
            send(source.at[z_rows(me.wrap(me.z + d, me.Z), 0)], into.at[d], z_send.at[kind, d], z_recv.at[kind, d], me.along_z(d))

    def z_collect(kind, source, into):
        total = source[z_rows(me.z, 0), :]
        for d in range(1, me.Z):
            remote(into.at[d], into.at[d], z_send.at[kind, d], z_recv.at[kind, d], me.along_z(d)).wait_recv()
            total = total + into[d]
        return total

    def share(part, f):
        rows = part.shape[0] // me.F
        start = f * rows
        return part.at[pl.ds(start if len(part.shape) == 3 else pl.multiple_of(start, 8), rows)]

    def spread(kind, here):
        for d in range(1, me.F):
            send(here, here, f_send.at[kind, d], f_recv.at[kind, d], me.fsdp(d))

    def scatter(kind, part, into):
        for d in range(1, me.F):
            send(share(part, me.wrap(me.f + d, me.F)), into.at[d], f_send.at[kind, d], f_recv.at[kind, d], me.fsdp(d))

    def collect(kind, part, into, result):
        total = share(part, me.f)[...]
        for d in range(1, me.F):
            remote(into.at[d], into.at[d], f_send.at[kind, d], f_recv.at[kind, d], me.fsdp(d)).wait_recv()
            total = total + into[d]
        here = share(result, me.f)
        here[...] = total
        spread(kind + 1, here)

    def arrive(kind, result):
        for d in range(1, me.F):
            there = share(result, me.wrap(me.f - d, me.F))
            remote(there, there, f_send.at[kind, d], f_recv.at[kind, d], me.fsdp(d)).wait_recv()

    core_swap(0, mixed.at[other], mixed_in)
    loads[4].wait()
    partial[...] = dot(blended_ref[...], basis_ref[...])
    pump(WHEN[0])
    core_here(0, mixed_in)
    mixed_half[...] = mixed[mine, :] + mixed_in[...]
    z_scatter(0, mixed_half, mixed_z)
    pump(WHEN[1])
    own = mixed_all.at[pl.ds(me.f, 1)]
    own[0] = z_collect(0, mixed_half, mixed_z)
    spread(0, own)
    pump(WHEN[2])
    arrive(0, mixed_all)
    assert features_here()
    which = lax.broadcasted_iota(jnp.int32, (TAPS, 3 * RANK), 0) // piece

    def add_mixed(pair, carry):
        left, right = [], []
        for i in range(2):
            columns = pl.ds(pl.multiple_of(i * 2 * TAPS + me.c * TAPS, TAPS), TAPS)
            left.append(features[pair, :, columns])
            terms = in_three(mixed_all[2 * pair + i]).astype(jnp.float32)
            right.append(jnp.where(which == me.z, jnp.concatenate([terms] * me.Z, axis=0), 0.0).astype(jnp.bfloat16))
        partial[...] += three_dot(jnp.concatenate(left, axis=1), jnp.concatenate(right, axis=0))
        return carry

    lax.fori_loop(0, me.F // 2, add_mixed, 0)
    core_swap(1, partial.at[other], half_in)
    adding.append(True)
    pump(WHEN[3])
    core_here(1, half_in)
    half_sum[...] = partial[mine, :] + half_in[...]
    z_scatter(1, half_sum, z_in)
    pump(WHEN[4])
    held = z_rows(me.z, me.c * half)
    sketch_ref[held, :] = z_collect(1, half_sum, z_in)
    for d in range(1, me.Z):
        send(sketch_ref.at[held], sketch_ref.at[held], z_send.at[2, d], z_recv.at[2, d], me.along_z(d))
    pump(WHEN[5])
    for d in range(1, me.Z):
        there = sketch_ref.at[z_rows(me.wrap(me.z - d, me.Z), me.c * half)]
        remote(there, there, z_send.at[2, d], z_recv.at[2, d], me.along_z(d)).wait_recv()
    core_swap(2, sketch_ref.at[mine], sketch_ref.at[mine])
    pump(WHEN[6])
    core_here(2, sketch_ref.at[other])
    core_half = sketch_ref[:, pl.ds(pl.multiple_of(me.c * 128, 128), 128)]
    gram = rows_dot(core_half, sketch_ref[...])
    for i in range(16):
        for j in range(2):
            gram_part[2 * i + j] = gram[8 * i : 8 * i + 8, 128 * j : 128 * j + 128]
    scatter(1, gram_part, gram_in)
    pump(WHEN[7])
    gram_mine = gram_all.at[me.c]
    collect(1, gram_part, gram_in, gram_mine)
    pump(1e9)
    while ready:
        add(*ready.pop(0))
    right_part[...] = rows_dot(blended_ref[...], sketch_ref[...])
    scatter(3, right_part, right_in)
    for m in order:
        copy_of(m, False).wait_send()
    arrive(2, gram_mine)
    core_swap(3, gram_mine, gram_mine)
    core_here(3, gram_all.at[1 - me.c])

    top = jnp.concatenate(inverse_factor([gram_all[0, 2 * i] for i in range(16)]), axis=0)
    below = jnp.concatenate([gram_all[1, 2 * i] for i in range(16)], axis=0)
    lower = dot_t(below, top)
    rest = jnp.concatenate([gram_all[1, 2 * i + 1] for i in range(16)], axis=0) - dot_t(lower, lower)
    collect(3, right_part, right_in, right_ref)
    bottom = jnp.concatenate(inverse_factor(by_eight(rest)), axis=0)
    cross = -dot(bottom, dot(lower, top))
    inverse = jnp.concatenate([
        jnp.concatenate([top, jnp.zeros_like(top)], axis=1), jnp.concatenate([cross, bottom], axis=1)
    ], axis=0)
    arrive(4, right_ref)

    projected = dot_t(right_ref[...], inverse)
    projected_ref[...] = projected
    squares[0] = jnp.sum(projected * projected, axis=0, keepdims=True)
    for d in range(1, me.T):
        send(squares.at[0], squares.at[d], t_send.at[d], t_recv.at[d], me.tensor(d))
    orthonormal = dot_t(sketch_ref[...], inverse)
    orthonormal_ref[...] = orthonormal
    momentum_ref[...] = blended_ref[...] - (1.0 - momentum_decay) * dot_t(orthonormal, projected)
    total = squares[0]
    for d in range(1, me.T):
        remote(squares.at[d], squares.at[d], t_send.at[d], t_recv.at[d], me.tensor(d)).wait_recv()
        total = total + squares[d]
    scale_ref[...] = 1.0 / jnp.sqrt(total / D + epsilon)
    drain()


def finish_kernel(
    orthonormal_ref, projected_ref, momentum_ref, scale_ref, update_hbm, momentum_hbm, basis_hbm, update, basis, sems
):
    out = [pltpu.make_async_copy(momentum_ref, momentum_hbm, sems.at[0])]
    out[0].start()
    basis[...] = projected_ref[...] * scale_ref[...]
    out.append(pltpu.make_async_copy(basis, basis_hbm, sems.at[1]))
    out[1].start()
    update[...] = (math.sqrt(D / RANK) * dot_t(orthonormal_ref[...], basis[...])).astype(jnp.bfloat16)
    out.append(pltpu.make_async_copy(update, update_hbm, sems.at[2]))
    out[2].start()
    for copy in out:
        copy.wait()


def call(kernel, name, outs, scratch, collective, in_space, out_space, *args):
    params = dict(vmem_limit_bytes=56 << 20)
    if collective is not None:
        params.update(collective_id=collective, has_side_effects=True)
    return pl.pallas_call(
        kernel,
        name=name,
        out_shape=[jax.ShapeDtypeStruct(shape, dtype) for shape, dtype in outs],
        in_specs=[in_space] * len(args),
        out_specs=[out_space] * len(outs),
        scratch_shapes=scratch,
        compiler_params=pltpu.CompilerParams(**params),
        cost_estimate=pl.CostEstimate(flops=3 * 10**9, bytes_accessed=4 << 20, transcendentals=0),
    )(*args)


def shards(sizes, inputs, grad_out, filters, momentum, basis):
    X, Y, Z = sizes
    F, T = X * Y, 2 * Z
    dma = pltpu.SemaphoreType.DMA
    f32, bf16 = jnp.float32, jnp.bfloat16
    tokens, channels = grad_out.shape
    width = inputs.shape[1]
    messages, _, _ = plan(sizes)
    half = width // 2
    orthonormal, projected, momentum, scale = call(
        functools.partial(main_kernel, sizes), "main",
        [((width, RANK), f32), ((channels, RANK), f32), ((width, channels), f32), ((1, RANK), f32)],
        [
            pltpu.VMEM(inputs.shape, bf16), pltpu.VMEM(grad_out.shape, bf16), pltpu.VMEM(filters.shape, bf16),
            pltpu.VMEM(basis.shape, f32), pltpu.VMEM((width, channels), f32),
            pltpu.VMEM((TAPS, channels), bf16),
            pltpu.VMEM((filters.shape[0] * TAPS, 2 * TAPS), bf16),
            pltpu.VMEM((X, Y, HALF, channels), bf16),
            pltpu.VMEM((Y, X, HALF, channels), bf16),
            pltpu.VMEM((T, width, inputs.shape[0]), bf16),
            pltpu.VMEM((tokens, RANK), f32), pltpu.VMEM((TAPS, RANK), f32), pltpu.VMEM((TAPS, RANK), f32),
            pltpu.VMEM((Z, TAPS // Z, RANK), f32), pltpu.VMEM((F, TAPS // Z, RANK), f32),
            pltpu.VMEM((width, RANK), f32), pltpu.VMEM((half, RANK), f32), pltpu.VMEM((half, RANK), f32),
            pltpu.VMEM((Z, half // Z, RANK), f32), pltpu.VMEM((width, RANK), f32),
            pltpu.VMEM((32, 8, 128), f32), pltpu.VMEM((F, 32 // F, 8, 128), f32), pltpu.VMEM((2, 32, 8, 128), f32),
            pltpu.VMEM((channels, RANK), f32), pltpu.VMEM((F, channels // F, RANK), f32), pltpu.VMEM((channels, RANK), f32),
            pltpu.VMEM((T, 1, RANK), f32),
            dma((5,)), dma((2,)), dma((len(messages),)), dma((len(messages),)), dma((4, 2)),
            dma((3, Z)), dma((3, Z)), dma((5, F)), dma((5, F)), dma((T,)), dma((T,)),
        ],
        1, ANY, VMEM, inputs, grad_out, filters, momentum, basis,
    )
    return tuple(call(
        finish_kernel, "finish",
        [((width, channels), bf16), ((width, channels), f32), ((channels, RANK), f32)],
        [pltpu.VMEM((width, channels), bf16), pltpu.VMEM((channels, RANK), f32), dma((3,))],
        None, VMEM, ANY, orthonormal, projected, momentum, scale,
    ))


def solution(mesh):
    fsdp, tensor = mesh.shape["fsdp"], mesh.shape["tensor"]
    X = 4 if fsdp == 32 else 2
    placed = (
        P("tensor", "fsdp"),
        P("fsdp", "tensor"),
        P("tensor", None),
        P("fsdp", "tensor"),
        P("tensor", None),
    )
    return jax.shard_map(
        functools.partial(shards, (X, fsdp // X, tensor // 2)),
        mesh=mesh,
        in_specs=placed,
        out_specs=(P("fsdp", "tensor"), P("fsdp", "tensor"), P("tensor", None)),
        check_vma=False,
    )
```

```python
import functools
import math

import jax
import jax.numpy as jnp
from jax import lax
from jax.experimental import pallas as pl
from jax.experimental.pallas import tpu as pltpu
from jax.sharding import PartitionSpec as P

D = 8192
GROUP = 16
RANK = 256
TAPS = 128
HALF = 128

WHEN = (10.0, 15.0, 21.0, 26.0, 33.0, 38.0, 39.5, 47.0, 52.0)

momentum_decay = 0.95
epsilon = 1e-06

MESH = pl.DeviceIdType.MESH
HIGHEST = lax.Precision.HIGHEST
VMEM = pl.BlockSpec(memory_space=pltpu.VMEM)
ANY = pl.BlockSpec(memory_space=pl.ANY)


class Place:
    def __init__(self, sizes):
        self.X, self.Y, self.Z = sizes
        self.F, self.T = self.X * self.Y, self.Z * 2
        self.f, self.t = lax.axis_index("fsdp"), lax.axis_index("tensor")
        self.y, self.x = self.f // self.X, lax.rem(self.f, self.X)
        self.z, self.c = self.t // 2, lax.rem(self.t, 2)

    def wrap(self, value, n):
        return lax.rem(value + 2 * n, n)

    def plane(self, dy, dx):
        return (self.wrap(self.y + dy, self.Y) * self.X + self.wrap(self.x + dx, self.X), self.t)

    def along_z(self, dz):
        return (self.f, self.wrap(self.z + dz, self.Z) * 2 + self.c)

    def sibling(self):
        return (self.f, self.z * 2 + 1 - self.c)

    def fsdp(self, d):
        return (self.wrap(self.f + d, self.F), self.t)

    def tensor(self, d):
        return (self.f, self.wrap(self.t + d, self.T))


def greet(peers):
    barrier = pltpu.get_barrier_semaphore()
    for peer in peers:
        pl.semaphore_signal(barrier, inc=1, device_id=peer, device_id_type=MESH)


def all_greeted(peers):
    pl.semaphore_wait(pltpu.get_barrier_semaphore(), len(peers))


def remote(src, dst, send, recv, peer):
    return pltpu.make_async_remote_copy(
        src_ref=src, dst_ref=dst, send_sem=send, recv_sem=recv, device_id=peer, device_id_type=MESH
    )


def ring(n, axis, rows, tell, first):
    lo, count = rows
    half = n // 2
    pieces = [(0, rows, first)]
    for sign in (1, -1):
        before = first
        for step in range(1, half + 1):
            part = rows
            if step == half:
                part = (lo, count // 2) if sign > 0 else (lo + count // 2, count // 2)
            before = tell(axis, sign, sign * (step - 1), part, before)
            pieces.append((sign * step, part, before))
    return pieces


def plan(sizes):
    X, Y, Z = sizes
    messages = []

    def teller(part, fixed):
        def tell(axis, sign, offset, rows, needs):
            where = dict(fixed)
            where[axis] = offset
            messages.append(dict(part=part, axis=axis, sign=sign, at=where, rows=rows, needs=needs))
            return len(messages) - 1

        return tell

    quarter = HALF // 4
    for sign in (1, -1):
        tell = teller("A", {"y": 0})
        near = tell("x", sign, 0, (0, HALF), "A")
        rows = (2 * quarter if sign > 0 else 3 * quarter, quarter)
        ring(Y, "y", rows, teller("A", {"x": 2 * sign}), tell("x", sign, sign, rows, near))
        for oy, rows, needs in ring(Y, "y", (0, HALF), teller("A", {"x": sign}), near):
            if rows[0] == 0:
                far = (0 if sign > 0 else quarter, quarter)
                teller("A", {"y": oy})("x", sign, sign, far, needs)
    ring(Y, "y", (0, HALF), teller("A", {"x": 0}), "A")
    for oy, rows, needs in ring(Y, "y", (0, HALF), teller("B", {"x": 0}), "B"):
        ring(X, "x", rows, teller("B", {"y": oy}), needs)
    for oz, rows, needs in ring(Z, "z", (0, 256), teller("I", {}), "I"):
        teller("I", {"z": oz})("c", 1, 0, rows, needs)
    ready = {"I": 0.3, "B": 2.5, "A": 5.5}
    free, arrival = {}, {}
    waiting = list(range(len(messages)))
    while waiting:
        when = {m: ready[messages[m]["needs"]] for m in waiting if messages[m]["needs"] in ready}
        best = min(when, key=lambda m: (max(when[m], free.get((messages[m]["axis"], messages[m]["sign"]), 0)), when[m], m))
        message = messages[best]
        link = (message["axis"], message["sign"])
        start = max(when[best], free.get(link, 0.0))
        length = message["rows"][1] * 1024 * (2 / 1e5 if link[0] != "c" else 1 / 4e5)
        free[link] = start + length
        ready[best] = arrival[best] = start + length + 1.8
        message["starts"] = start
        waiting.remove(best)
    order = sorted(arrival, key=lambda m: arrival[m])
    return messages, order, arrival


def strided_taps(filters, toeplitz_ref):
    shape = (TAPS, TAPS)
    upper = lax.broadcasted_iota(jnp.int32, shape, 1) >= lax.broadcasted_iota(jnp.int32, shape, 0)
    for g in range(filters.shape[0]):
        rolled = pltpu.roll(jnp.broadcast_to(filters[g : g + 1, :], shape), 0, 1, stride=1, stride_axis=0)
        rows = pl.ds(g * TAPS, TAPS)
        toeplitz_ref[rows, :TAPS] = jnp.where(upper, rolled, 0.0).astype(jnp.bfloat16)
        toeplitz_ref[rows, TAPS:] = jnp.where(upper, 0.0, rolled).astype(jnp.bfloat16)


def convolve(toeplitz_ref, window):
    channels = window.shape[1]
    group = lax.broadcasted_iota(jnp.int32, (TAPS, 128), 1) // GROUP
    each = 128 // GROUP
    columns = []
    for q in range(channels // 128):
        product = jnp.dot(
            toeplitz_ref[q * each * TAPS : (q + 1) * each * TAPS, :],
            window[:, q * 128 : (q + 1) * 128],
            preferred_element_type=jnp.float32,
        )
        total = product[:TAPS]
        for i in range(1, each):
            total = jnp.where(group == i, product[i * TAPS : (i + 1) * TAPS], total)
        columns.append(total)
    return jnp.concatenate(columns, axis=1).astype(jnp.bfloat16)


def rows_dot(left, right):
    return lax.dot_general(
        left, right, (((0,), (0,)), ((), ())), precision=HIGHEST, preferred_element_type=jnp.float32
    )


def dot_t(left, right):
    return lax.dot_general(
        left, right, (((1,), (1,)), ((), ())), precision=HIGHEST, preferred_element_type=jnp.float32
    )


def dot(left, right):
    return jnp.dot(left, right, precision=HIGHEST, preferred_element_type=jnp.float32)


def inverse_factor(rows):
    shape = (8, 128)
    rows = list(rows)
    lane = lax.broadcasted_iota(jnp.int32, shape, 1)
    sub = lax.broadcasted_iota(jnp.int32, shape, 0)

    def column(value, k):
        return jnp.broadcast_to(value[:, k : k + 1], shape)

    def row(value, k):
        return jnp.broadcast_to(value[k : k + 1, :], shape)

    for b in range(len(rows)):
        base = 8 * b
        pivot = rows[b]
        columns = [column(pivot, base + j) for j in range(8)]
        inside = (lane >= base) & (lane < base + 8)
        pivot = jnp.where(inside, jnp.where(lane - base == sub, 1.0, 0.0), pivot)
        scale = jnp.zeros(shape, jnp.float32)
        inverses, uppers, crossed = [], [], {}
        for j in range(8):
            diagonal = row(columns[j], j)
            inverse = 1.0 / diagonal
            lower = jnp.where(sub > j, columns[j] * inverse, 0.0)
            scale = jnp.where(sub == j, lax.rsqrt(diagonal), scale)
            for k in range(j + 1, 8):
                crossed[j, k] = row(columns[k], j)
                columns[k] = columns[k] - lower * crossed[j, k]
            upper = row(pivot, j)
            pivot = pivot - lower * upper
            inverses.append(inverse)
            uppers.append(upper)
        rows[b] = jnp.where(lane < base + 8, pivot * scale, 0.0)
        for i in range(b + 1, len(rows)):
            below = rows[i]
            columns = [column(below, base + j) for j in range(8)]
            below = jnp.where(inside, 0.0, below)
            for j in range(8):
                lower = columns[j] * inverses[j]
                for k in range(j + 1, 8):
                    columns[k] = columns[k] - lower * crossed[j, k]
                below = below - lower * uppers[j]
            rows[i] = below
    return rows


def by_eight(block):
    return [block[8 * i : 8 * i + 8, :] for i in range(block.shape[0] // 8)]


def in_three(value):
    high = value.astype(jnp.bfloat16)
    rest = value - high.astype(jnp.float32)
    middle = rest.astype(jnp.bfloat16)
    low = (rest - middle.astype(jnp.float32)).astype(jnp.bfloat16)
    return jnp.concatenate([high, middle, low], axis=1)


def three_dot(left, right):
    n = right.shape[1] // 3
    product = jnp.dot(left, right, preferred_element_type=jnp.float32)
    return product[:, :n] + (product[:, n : 2 * n] + product[:, 2 * n :])


def main_kernel(
    sizes, inputs_hbm, grad_hbm, filters_hbm, momentum_hbm, basis_hbm,
    orthonormal_ref, projected_ref, momentum_ref, scale_ref,
    inputs_ref, grad_ref, filters_ref, basis_ref, blended_ref,
    halo, toeplitz, first, second, features,
    mixed, mixed_in, mixed_half, mixed_z, mixed_all,
    partial, half_in, half_sum, z_in, part, part_in, sketch_ref,
    gram_part, gram_in, gram_all, right_part, right_x, right_mid, right_y, right_ref, squares,
    load_sem, halo_sem, send_sem, recv_sem, core_sem, z_send, z_recv, f_send, f_recv, p_send, p_recv, t_send, t_recv,
):
    me = Place(sizes)
    loads = [
        pltpu.make_async_copy(there, here, load_sem.at[i])
        for i, (there, here) in enumerate([
            (inputs_hbm, inputs_ref), (grad_hbm, grad_ref), (filters_hbm, filters_ref),
            (basis_hbm, basis_ref), (momentum_hbm, blended_ref),
        ])
    ]
    for load in loads:
        load.start()
    peers = [me.fsdp(d) for d in range(1, me.F)] + [me.tensor(d) for d in range(1, me.T)]
    greet(peers)
    messages, order, arrival = plan(sizes)
    loads[0].wait()
    features[me.t] = jnp.transpose(inputs_ref[...].astype(jnp.float32)).astype(jnp.bfloat16)
    loads[1].wait()
    all_greeted(peers)

    def copy_of(m, arriving):
        message = messages[m]
        sign = message["sign"]
        shift = sign if arriving else 0
        at, axis = dict(message["at"]), message["axis"]
        rows = pl.ds(*message["rows"])
        if axis in at:
            at[axis] += shift
        if message["part"] == "I":
            core = me.c
            if axis == "c" and arriving:
                core = 1 - me.c
            block = features.at[me.wrap(me.z - at["z"], me.Z) * 2 + core, rows]
            peer = me.sibling() if axis == "c" else me.along_z(sign)
        else:
            y, x = me.wrap(me.y - at["y"], me.Y), me.wrap(me.x - at["x"], me.X)
            block = second.at[y, x, rows] if message["part"] == "A" else first.at[x, y, rows]
            peer = me.plane(0, sign) if axis == "x" else me.plane(sign, 0)
        return remote(block, block, send_sem.at[m], recv_sem.at[m], peer)

    def start_after(event):
        for m in sorted((m for m in range(len(messages)) if messages[m]["needs"] == event), key=lambda m: messages[m]["starts"]):
            copy_of(m, False).start()

    def add(oy, ox):
        y, x = me.wrap(me.y - oy, me.Y), me.wrap(me.x - ox, me.X)
        f = y * me.X + x
        rows = jnp.concatenate([first[x, y], second[y, x]], axis=0)
        columns = pl.ds(pl.multiple_of(lax.rem(f, 2) * 2 * TAPS, 2 * TAPS), 2 * TAPS)
        blended_ref[...] += jnp.dot(features[f // 2, :, columns], rows, preferred_element_type=jnp.float32)

    have = {(part, 0, 0): HALF for part in "AB"}
    ready, pending = [(0, 0)], list(order)
    adding = []

    def features_here():
        return not any(messages[m]["part"] == "I" for m in pending)

    def pump(until):
        while pending and arrival[pending[0]] <= until:
            m = pending.pop(0)
            copy_of(m, True).wait_recv()
            start_after(m)
            message = messages[m]
            if message["part"] != "I":
                at = dict(message["at"])
                at[message["axis"]] += message["sign"]
                place = (at["y"] % me.Y, at["x"] % me.X)
                have[(message["part"],) + place] = have.get((message["part"],) + place, 0) + message["rows"][1]
                if have.get(("A",) + place) == HALF and have.get(("B",) + place) == HALF:
                    ready.append(place)
            for _ in range(2):
                if adding and features_here() and ready:
                    add(*ready.pop(0))

    out = []

    def send(*args):
        out.append(remote(*args))
        out[-1].start()

    def drain():
        for copy in out:
            copy.wait_send()
        out.clear()

    send(grad_ref.at[pl.ds(0, TAPS)], halo, halo_sem.at[0], halo_sem.at[1], me.fsdp(-1))
    start_after("I")
    loads[2].wait()
    strided_taps(filters_ref[...].astype(jnp.float32), toeplitz)
    first[me.x, me.y] = convolve(toeplitz, grad_ref[...])
    start_after("B")
    loads[3].wait()
    basis_terms = in_three(jnp.transpose(basis_ref[...]))

    def times_basis(rows):
        product = 0.0
        for i in range(3):
            term = basis_terms[:, i * rows.shape[1] : (i + 1) * rows.shape[1]]
            product += lax.dot_general(term, rows, (((1,), (1,)), ((), ())), preferred_element_type=jnp.float32)
        return product

    mixed[0] = times_basis(first[me.x, me.y])
    out[0].wait_recv()
    tail = jnp.where(me.f == me.F - 1, jnp.zeros_like(halo[...]), halo[...])
    second[me.y, me.x] = convolve(toeplitz, jnp.concatenate([grad_ref[TAPS:, :], tail], axis=0))
    start_after("A")
    mixed[1] = times_basis(second[me.y, me.x])

    piece = RANK // me.Z
    small = piece // 2

    def core_swap(kind, there, here):
        send(there, here, core_sem.at[kind, 0], core_sem.at[kind, 1], me.sibling())

    def core_here(kind, here):
        remote(here, here, core_sem.at[kind, 0], core_sem.at[kind, 1], me.sibling()).wait_recv()

    def z_scatter(kind, source, into):
        for d in range(1, me.Z):
            send(source.at[me.wrap(me.z + d, me.Z)], into.at[d], z_send.at[kind, d], z_recv.at[kind, d], me.along_z(d))

    def z_collect(kind, source, into):
        total = source[me.z]
        for d in range(1, me.Z):
            remote(into.at[d], into.at[d], z_send.at[kind, d], z_recv.at[kind, d], me.along_z(d)).wait_recv()
            total = total + into[d]
        return total

    def share(part, f):
        rows = part.shape[0] // me.F
        start = f * rows
        return part.at[pl.ds(start if len(part.shape) == 3 else pl.multiple_of(start, 8), rows)]

    def scatter(kind, part, into):
        for d in range(1, me.F):
            send(share(part, me.wrap(me.f + d, me.F)), into.at[d], f_send.at[kind, d], f_recv.at[kind, d], me.fsdp(d))

    def collect(kind, part, into):
        total = share(part, me.f)[...]
        for d in range(1, me.F):
            remote(into.at[d], into.at[d], f_send.at[kind, d], f_recv.at[kind, d], me.fsdp(d)).wait_recv()
            total = total + into[d]
        return total


    def gather_y(kind, block):
        here = block(me.y, me.x)
        for dy in range(1, me.Y):
            send(here, here, p_send.at[kind, 0, dy], p_recv.at[kind, 0, dy], me.plane(dy, 0))
        for dx in range(1, me.X):
            send(here, here, p_send.at[kind, dx, 0], p_recv.at[kind, dx, 0], me.plane(0, dx))

    def gather_x(kind, block):
        for dy in sorted(range(1, me.Y), key=lambda d: min(d, me.Y - d)):
            there = block(me.wrap(me.y - dy, me.Y), me.x)
            remote(there, there, p_send.at[kind, 0, dy], p_recv.at[kind, 0, dy], me.plane(dy, 0)).wait_recv()
            for dx in range(1, me.X):
                send(there, there, p_send.at[kind, dx, dy], p_recv.at[kind, dx, dy], me.plane(0, dx))

    def gathered(kind, block, columns=None):
        for dx in columns or range(1, me.X):
            for dy in range(me.Y):
                there = block(me.wrap(me.y - dy, me.Y), me.wrap(me.x - dx, me.X))
                remote(there, there, p_send.at[kind, dx, dy], p_recv.at[kind, dx, dy], me.plane(0, dx)).wait_recv()

    core_swap(0, mixed.at[1 - me.c], mixed_in)
    loads[4].wait()
    from_momentum = lax.dot_general(
        jnp.transpose(basis_ref[...]), blended_ref[...], (((1,), (1,)), ((), ())),
        precision=HIGHEST, preferred_element_type=jnp.float32,
    )
    for z in range(me.Z):
        for c in range(2):
            at = z * piece + c * small
            partial[c, z] = from_momentum[at : at + small, :]
    core_here(0, mixed_in)
    for z in range(me.Z):
        rows = slice(z * piece, (z + 1) * piece)
        mixed_half[z] = mixed[me.c, rows, :] + mixed_in[rows, :]
    z_scatter(0, mixed_half, mixed_z)
    core_swap(1, partial.at[1 - me.c], half_in)
    pump(WHEN[0])
    core_here(1, half_in)
    half_sum[...] = partial[me.c] + half_in[...]
    pump(WHEN[1])
    mixed_all[me.f] = z_collect(0, mixed_half, mixed_z)

    def mixed_block(y, x):
        return mixed_all.at[y * me.X + x]

    gather_y(0, mixed_block)
    z_scatter(1, half_sum, z_in)
    pump(WHEN[2])
    gather_x(0, mixed_block)
    pump(WHEN[3])
    held = z_collect(1, half_sum, z_in)
    gathered(0, mixed_block)
    while not features_here():
        pump(arrival[pending[0]])

    def add_mixed(pair, total):
        left = jnp.concatenate([mixed_all[2 * pair], mixed_all[2 * pair + 1]], axis=1)
        high = left.astype(jnp.bfloat16)
        rest = left - high.astype(jnp.float32)
        middle = rest.astype(jnp.bfloat16)
        low = (rest - middle.astype(jnp.float32)).astype(jnp.bfloat16)
        columns = [pl.ds(pl.multiple_of(i * 2 * TAPS + me.c * TAPS, TAPS), TAPS) for i in range(2)]
        right = jnp.concatenate([features[pair, :, column] for column in columns], axis=1)
        return total + lax.dot_general(
            jnp.concatenate([high, middle, low], axis=0), right, (((1,), (1,)), ((), ())), preferred_element_type=jnp.float32
        )

    total = lax.fori_loop(0, me.F // 2, add_mixed, jnp.zeros((3 * piece, features.shape[1]), jnp.float32))
    total = total[:piece] + (total[piece : 2 * piece] + total[2 * piece :])
    part[0] = total[:small]
    part[1] = total[small:]
    core_swap(2, part.at[1 - me.c], part_in)
    adding.append(True)
    pump(WHEN[4])
    core_here(2, part_in)
    own = sketch_ref.at[me.c, me.z]
    own[...] = held + (part[me.c] + part_in[...])
    for d in range(1, me.Z):
        send(own, own, z_send.at[2, d], z_recv.at[2, d], me.along_z(d))
    pump(WHEN[5])
    for d in range(1, me.Z):
        there = sketch_ref.at[me.c, me.wrap(me.z - d, me.Z)]
        remote(there, there, z_send.at[2, d], z_recv.at[2, d], me.along_z(d)).wait_recv()
    core_swap(3, sketch_ref.at[me.c], sketch_ref.at[me.c])
    pump(WHEN[6])
    core_here(3, sketch_ref.at[1 - me.c])
    sketch_t = jnp.concatenate([sketch_ref[c, z] for z in range(me.Z) for c in range(2)], axis=0)
    gram = dot_t(sketch_t, sketch_t)
    for c in range(2):
        @pl.when(me.c == c)
        def _():
            for i in range(16):
                for j in range(2):
                    at = 128 * c + 8 * i
                    gram_part[2 * i + j] = gram[at : at + 8, 128 * j : 128 * j + 128]
    scatter(0, gram_part, gram_in)
    sketch = jnp.transpose(sketch_t)
    pump(WHEN[7])
    gram_mine = gram_all.at[me.c]

    def gram_block(y, x):
        return share(gram_mine, y * me.X + x)

    gram_block(me.y, me.x)[...] = collect(0, gram_part, gram_in)
    gather_y(3, gram_block)
    pump(WHEN[8])
    gather_x(3, gram_block)
    pump(1e9)
    while ready:
        add(*ready.pop(0))
    right_part[...] = rows_dot(blended_ref[...], sketch)
    column = right_part.shape[0] // me.X
    block_rows = column // me.Y

    def right_column(x):
        return pl.ds(pl.multiple_of(x * column, 8), column)

    def right_block(y, x):
        return right_ref.at[pl.ds(pl.multiple_of(x * column + y * block_rows, 8), block_rows)]

    for dx in range(1, me.X):
        send(right_part.at[right_column(me.wrap(me.x + dx, me.X))], right_x.at[dx], p_send.at[1, dx, 0], p_recv.at[1, dx, 0], me.plane(0, dx))
    for m in order:
        copy_of(m, False).wait_send()
    gathered(3, gram_block)
    core_swap(4, gram_mine, gram_mine)
    total = right_part[right_column(me.x), :]
    for dx in range(1, me.X):
        remote(right_x.at[dx], right_x.at[dx], p_send.at[1, dx, 0], p_recv.at[1, dx, 0], me.plane(0, dx)).wait_recv()
        total = total + right_x[dx]
    right_mid[...] = total

    def middle_rows(y):
        return pl.ds(pl.multiple_of(y * block_rows, 8), block_rows)

    for dy in range(1, me.Y):
        send(right_mid.at[middle_rows(me.wrap(me.y + dy, me.Y))], right_y.at[dy], p_send.at[1, 0, dy], p_recv.at[1, 0, dy], me.plane(dy, 0))
    core_here(4, gram_all.at[1 - me.c])

    top = jnp.concatenate(inverse_factor([gram_all[0, 2 * i] for i in range(16)]), axis=0)
    total = right_mid[middle_rows(me.y), :]
    for dy in range(1, me.Y):
        remote(right_y.at[dy], right_y.at[dy], p_send.at[1, 0, dy], p_recv.at[1, 0, dy], me.plane(dy, 0)).wait_recv()
        total = total + right_y[dy]
    right_block(me.y, me.x)[...] = total
    gather_y(2, right_block)
    below = jnp.concatenate([gram_all[1, 2 * i] for i in range(16)], axis=0)
    lower = dot_t(below, top)
    rest = jnp.concatenate([gram_all[1, 2 * i + 1] for i in range(16)], axis=0) - dot_t(lower, lower)
    bottom = jnp.concatenate(inverse_factor(by_eight(rest)), axis=0)
    gather_x(2, right_block)
    cross = -dot(bottom, dot(lower, top))
    inverse = jnp.concatenate([
        jnp.concatenate([top, jnp.zeros_like(top)], axis=1), jnp.concatenate([cross, bottom], axis=1)
    ], axis=0)
    orthonormal = dot_t(sketch, inverse)
    orthonormal_ref[...] = orthonormal
    drain()
    total = 0.0
    for dx in sorted(range(me.X), key=lambda d: min(d, me.X - d)):
        if dx:
            gathered(2, right_block, [dx])
        rows = right_column(me.wrap(me.x - dx, me.X))
        projected = dot_t(right_ref[rows, :], inverse)
        projected_ref[rows, :] = projected
        total += jnp.sum(projected * projected, axis=0, keepdims=True)
    squares[0] = total
    for d in range(1, me.T):
        send(squares.at[0], squares.at[d], t_send.at[d], t_recv.at[d], me.tensor(d))
    momentum_ref[...] = blended_ref[...] - (1.0 - momentum_decay) * dot_t(orthonormal, projected_ref[...])
    total = squares[0]
    for d in range(1, me.T):
        remote(squares.at[d], squares.at[d], t_send.at[d], t_recv.at[d], me.tensor(d)).wait_recv()
        total = total + squares[d]
    scale_ref[...] = 1.0 / jnp.sqrt(total / D + epsilon)
    drain()


def finish_kernel(
    orthonormal_ref, projected_ref, momentum_ref, scale_ref, update_hbm, momentum_hbm, basis_hbm, update, basis, sems
):
    out = [pltpu.make_async_copy(momentum_ref, momentum_hbm, sems.at[0])]
    out[0].start()
    basis[...] = projected_ref[...] * scale_ref[...]
    out.append(pltpu.make_async_copy(basis, basis_hbm, sems.at[1]))
    out[1].start()
    update[...] = (math.sqrt(D / RANK) * dot_t(orthonormal_ref[...], basis[...])).astype(jnp.bfloat16)
    out.append(pltpu.make_async_copy(update, update_hbm, sems.at[2]))
    out[2].start()
    for copy in out:
        copy.wait()


def call(kernel, name, outs, scratch, collective, in_space, out_space, *args):
    params = dict(vmem_limit_bytes=56 << 20)
    if collective is not None:
        params.update(collective_id=collective, has_side_effects=True)
    return pl.pallas_call(
        kernel,
        name=name,
        out_shape=[jax.ShapeDtypeStruct(shape, dtype) for shape, dtype in outs],
        in_specs=[in_space] * len(args),
        out_specs=[out_space] * len(outs),
        scratch_shapes=scratch,
        compiler_params=pltpu.CompilerParams(**params),
        cost_estimate=pl.CostEstimate(flops=3 * 10**9, bytes_accessed=4 << 20, transcendentals=0),
    )(*args)


def shards(sizes, inputs, grad_out, filters, momentum, basis):
    X, Y, Z = sizes
    F, T = X * Y, 2 * Z
    dma = pltpu.SemaphoreType.DMA
    f32, bf16 = jnp.float32, jnp.bfloat16
    tokens, channels = grad_out.shape
    width = inputs.shape[1]
    messages, _, _ = plan(sizes)
    orthonormal, projected, momentum, scale = call(
        functools.partial(main_kernel, sizes), "main",
        [((width, RANK), f32), ((channels, RANK), f32), ((width, channels), f32), ((1, RANK), f32)],
        [
            pltpu.VMEM(inputs.shape, bf16), pltpu.VMEM(grad_out.shape, bf16), pltpu.VMEM(filters.shape, bf16),
            pltpu.VMEM(basis.shape, f32), pltpu.VMEM((width, channels), f32),
            pltpu.VMEM((TAPS, channels), bf16),
            pltpu.VMEM((filters.shape[0] * TAPS, 2 * TAPS), bf16),
            pltpu.VMEM((X, Y, HALF, channels), bf16),
            pltpu.VMEM((Y, X, HALF, channels), bf16),
            pltpu.VMEM((T, width, inputs.shape[0]), bf16),
            pltpu.VMEM((2, RANK, TAPS), f32), pltpu.VMEM((RANK, TAPS), f32), pltpu.VMEM((Z, RANK // Z, TAPS), f32),
            pltpu.VMEM((Z, RANK // Z, TAPS), f32), pltpu.VMEM((F, RANK // Z, TAPS), f32),
            pltpu.VMEM((2, Z, RANK // T, width), f32), pltpu.VMEM((Z, RANK // T, width), f32),
            pltpu.VMEM((Z, RANK // T, width), f32), pltpu.VMEM((Z, RANK // T, width), f32),
            pltpu.VMEM((2, RANK // T, width), f32), pltpu.VMEM((RANK // T, width), f32), pltpu.VMEM((2, Z, RANK // T, width), f32),
            pltpu.VMEM((32, 8, 128), f32), pltpu.VMEM((F, 32 // F, 8, 128), f32), pltpu.VMEM((2, 32, 8, 128), f32),
            pltpu.VMEM((channels, RANK), f32), pltpu.VMEM((X, channels // X, RANK), f32), pltpu.VMEM((channels // X, RANK), f32),
            pltpu.VMEM((Y, channels // F, RANK), f32), pltpu.VMEM((channels, RANK), f32),
            pltpu.VMEM((T, 1, RANK), f32),
            dma((5,)), dma((2,)), dma((len(messages),)), dma((len(messages),)), dma((5, 2)),
            dma((3, Z)), dma((3, Z)), dma((1, F)), dma((1, F)), dma((4, X, Y)), dma((4, X, Y)), dma((T,)), dma((T,)),
        ],
        1, ANY, VMEM, inputs, grad_out, filters, momentum, basis,
    )
    return tuple(call(
        finish_kernel, "finish",
        [((width, channels), bf16), ((width, channels), f32), ((channels, RANK), f32)],
        [pltpu.VMEM((width, channels), bf16), pltpu.VMEM((channels, RANK), f32), dma((3,))],
        None, VMEM, ANY, orthonormal, projected, momentum, scale,
    ))


def solution(mesh):
    fsdp, tensor = mesh.shape["fsdp"], mesh.shape["tensor"]
    X = 4 if fsdp == 32 else 2
    placed = (
        P("tensor", "fsdp"),
        P("fsdp", "tensor"),
        P("tensor", None),
        P("fsdp", "tensor"),
        P("tensor", None),
    )
    return jax.shard_map(
        functools.partial(shards, (X, fsdp // X, tensor // 2)),
        mesh=mesh,
        in_specs=placed,
        out_specs=(P("fsdp", "tensor"), P("fsdp", "tensor"), P("tensor", None)),
        check_vma=False,
    )
```

```python
import functools
import math

import jax
import jax.numpy as jnp
from jax import lax
from jax.experimental import pallas as pl
from jax.experimental.pallas import tpu as pltpu
from jax.sharding import PartitionSpec as P

D = 8192
GROUP = 16
RANK = 256
TAPS = 128
HALF = 128

WHEN = (10.0, 15.0, 21.0, 26.0, 33.0, 38.0, 39.5, 47.0, 52.0)

momentum_decay = 0.95
epsilon = 1e-06

MESH = pl.DeviceIdType.MESH
HIGHEST = lax.Precision.HIGHEST
VMEM = pl.BlockSpec(memory_space=pltpu.VMEM)
ANY = pl.BlockSpec(memory_space=pl.ANY)


class Place:
    def __init__(self, sizes):
        self.X, self.Y, self.Z = sizes
        self.F, self.T = self.X * self.Y, self.Z * 2
        self.f, self.t = lax.axis_index("fsdp"), lax.axis_index("tensor")
        self.y, self.x = self.f // self.X, lax.rem(self.f, self.X)
        self.z, self.c = self.t // 2, lax.rem(self.t, 2)

    def wrap(self, value, n):
        return lax.rem(value + 2 * n, n)

    def plane(self, dy, dx):
        return (self.wrap(self.y + dy, self.Y) * self.X + self.wrap(self.x + dx, self.X), self.t)

    def along_z(self, dz):
        return (self.f, self.wrap(self.z + dz, self.Z) * 2 + self.c)

    def sibling(self):
        return (self.f, self.z * 2 + 1 - self.c)

    def fsdp(self, d):
        return (self.wrap(self.f + d, self.F), self.t)

    def tensor(self, d):
        return (self.f, self.wrap(self.t + d, self.T))


def greet(peers):
    barrier = pltpu.get_barrier_semaphore()
    for peer in peers:
        pl.semaphore_signal(barrier, inc=1, device_id=peer, device_id_type=MESH)


def all_greeted(peers):
    pl.semaphore_wait(pltpu.get_barrier_semaphore(), len(peers))


def remote(src, dst, send, recv, peer):
    return pltpu.make_async_remote_copy(
        src_ref=src, dst_ref=dst, send_sem=send, recv_sem=recv, device_id=peer, device_id_type=MESH
    )


def ring(n, axis, rows, tell, first):
    lo, count = rows
    half = n // 2
    pieces = [(0, rows, first)]
    for sign in (1, -1):
        before = first
        for step in range(1, half + 1):
            part = rows
            if step == half:
                part = (lo, count // 2) if sign > 0 else (lo + count // 2, count // 2)
            before = tell(axis, sign, sign * (step - 1), part, before)
            pieces.append((sign * step, part, before))
    return pieces


def plan(sizes):
    X, Y, Z = sizes
    messages = []

    def teller(part, fixed):
        def tell(axis, sign, offset, rows, needs):
            where = dict(fixed)
            where[axis] = offset
            messages.append(dict(part=part, axis=axis, sign=sign, at=where, rows=rows, needs=needs))
            return len(messages) - 1

        return tell

    quarter = HALF // 4
    for sign in (1, -1):
        tell = teller("A", {"y": 0})
        near = tell("x", sign, 0, (0, HALF), "A")
        rows = (2 * quarter if sign > 0 else 3 * quarter, quarter)
        ring(Y, "y", rows, teller("A", {"x": 2 * sign}), tell("x", sign, sign, rows, near))
        for oy, rows, needs in ring(Y, "y", (0, HALF), teller("A", {"x": sign}), near):
            if rows[0] == 0:
                far = (0 if sign > 0 else quarter, quarter)
                teller("A", {"y": oy})("x", sign, sign, far, needs)
    ring(Y, "y", (0, HALF), teller("A", {"x": 0}), "A")
    for oy, rows, needs in ring(Y, "y", (0, HALF), teller("B", {"x": 0}), "B"):
        ring(X, "x", rows, teller("B", {"y": oy}), needs)
    for lo in (0, 128):
        for oz, rows, needs in ring(Z, "z", (lo, 128), teller("I", {}), "I"):
            teller("I", {"z": oz})("c", 1, 0, rows, needs)
    ready = {"I": 0.3, "B": 2.5, "A": 5.5}
    free, arrival = {}, {}
    waiting = list(range(len(messages)))
    while waiting:
        when = {m: ready[messages[m]["needs"]] for m in waiting if messages[m]["needs"] in ready}
        best = min(when, key=lambda m: (max(when[m], free.get((messages[m]["axis"], messages[m]["sign"]), 0)), when[m], m))
        message = messages[best]
        link = (message["axis"], message["sign"])
        start = max(when[best], free.get(link, 0.0))
        length = message["rows"][1] * 1024 * (2 / 1e5 if link[0] != "c" else 1 / 4e5)
        free[link] = start + length
        ready[best] = arrival[best] = start + length + 1.8
        message["starts"] = start
        waiting.remove(best)
    order = sorted(arrival, key=lambda m: arrival[m])
    return messages, order, arrival


def strided_taps(filters, toeplitz_ref):
    shape = (TAPS, TAPS)
    upper = lax.broadcasted_iota(jnp.int32, shape, 1) >= lax.broadcasted_iota(jnp.int32, shape, 0)
    for g in range(filters.shape[0]):
        rolled = pltpu.roll(jnp.broadcast_to(filters[g : g + 1, :], shape), 0, 1, stride=1, stride_axis=0)
        rows = pl.ds(g * TAPS, TAPS)
        toeplitz_ref[rows, :TAPS] = jnp.where(upper, rolled, 0.0).astype(jnp.bfloat16)
        toeplitz_ref[rows, TAPS:] = jnp.where(upper, 0.0, rolled).astype(jnp.bfloat16)


def convolve(toeplitz_ref, window):
    channels = window.shape[1]
    group = lax.broadcasted_iota(jnp.int32, (TAPS, 128), 1) // GROUP
    each = 128 // GROUP
    columns = []
    for q in range(channels // 128):
        product = jnp.dot(
            toeplitz_ref[q * each * TAPS : (q + 1) * each * TAPS, :],
            window[:, q * 128 : (q + 1) * 128],
            preferred_element_type=jnp.float32,
        )
        total = product[:TAPS]
        for i in range(1, each):
            total = jnp.where(group == i, product[i * TAPS : (i + 1) * TAPS], total)
        columns.append(total)
    return jnp.concatenate(columns, axis=1).astype(jnp.bfloat16)


def rows_dot(left, right):
    return lax.dot_general(
        left, right, (((0,), (0,)), ((), ())), precision=HIGHEST, preferred_element_type=jnp.float32
    )


def dot_t(left, right):
    return lax.dot_general(
        left, right, (((1,), (1,)), ((), ())), precision=HIGHEST, preferred_element_type=jnp.float32
    )


def dot(left, right):
    return jnp.dot(left, right, precision=HIGHEST, preferred_element_type=jnp.float32)


def inverse_factor(rows):
    shape = (8, 128)
    rows = list(rows)
    lane = lax.broadcasted_iota(jnp.int32, shape, 1)
    sub = lax.broadcasted_iota(jnp.int32, shape, 0)

    def column(value, k):
        return jnp.broadcast_to(value[:, k : k + 1], shape)

    def row(value, k):
        return jnp.broadcast_to(value[k : k + 1, :], shape)

    for b in range(len(rows)):
        base = 8 * b
        pivot = rows[b]
        columns = [column(pivot, base + j) for j in range(8)]
        inside = (lane >= base) & (lane < base + 8)
        pivot = jnp.where(inside, jnp.where(lane - base == sub, 1.0, 0.0), pivot)
        scale = jnp.zeros(shape, jnp.float32)
        inverses, uppers, crossed = [], [], {}
        for j in range(8):
            diagonal = row(columns[j], j)
            inverse = 1.0 / diagonal
            lower = jnp.where(sub > j, columns[j] * inverse, 0.0)
            scale = jnp.where(sub == j, lax.rsqrt(diagonal), scale)
            for k in range(j + 1, 8):
                crossed[j, k] = row(columns[k], j)
                columns[k] = columns[k] - lower * crossed[j, k]
            upper = row(pivot, j)
            pivot = pivot - lower * upper
            inverses.append(inverse)
            uppers.append(upper)
        rows[b] = jnp.where(lane < base + 8, pivot * scale, 0.0)
        for i in range(b + 1, len(rows)):
            below = rows[i]
            columns = [column(below, base + j) for j in range(8)]
            below = jnp.where(inside, 0.0, below)
            for j in range(8):
                lower = columns[j] * inverses[j]
                for k in range(j + 1, 8):
                    columns[k] = columns[k] - lower * crossed[j, k]
                below = below - lower * uppers[j]
            rows[i] = below
    return rows


def by_eight(block):
    return [block[8 * i : 8 * i + 8, :] for i in range(block.shape[0] // 8)]


def in_three(value):
    high = value.astype(jnp.bfloat16)
    rest = value - high.astype(jnp.float32)
    middle = rest.astype(jnp.bfloat16)
    low = (rest - middle.astype(jnp.float32)).astype(jnp.bfloat16)
    return jnp.concatenate([high, middle, low], axis=1)


def three_dot(left, right):
    n = right.shape[1] // 3
    product = jnp.dot(left, right, preferred_element_type=jnp.float32)
    return product[:, :n] + (product[:, n : 2 * n] + product[:, 2 * n :])


def main_kernel(
    sizes, inputs_hbm, grad_hbm, filters_hbm, momentum_hbm, basis_hbm,
    orthonormal_ref, projected_ref, momentum_ref, scale_ref,
    inputs_ref, grad_ref, filters_ref, basis_ref, blended_ref,
    halo, toeplitz, first, second, features,
    mixed, mixed_in, mixed_half, mixed_z, mixed_all,
    partial, half_in, half_sum, z_in, part, part_in, sketch_ref,
    gram_part, gram_in, gram_all, right_part, right_x, right_mid, right_y, right_ref, squares,
    load_sem, halo_sem, send_sem, recv_sem, core_sem, z_send, z_recv, f_send, f_recv, p_send, p_recv, t_send, t_recv,
):
    me = Place(sizes)
    loads = [
        pltpu.make_async_copy(there, here, load_sem.at[i])
        for i, (there, here) in enumerate([
            (inputs_hbm, inputs_ref), (grad_hbm, grad_ref), (filters_hbm, filters_ref),
            (basis_hbm, basis_ref), (momentum_hbm, blended_ref),
        ])
    ]
    for load in loads:
        load.start()
    peers = [me.fsdp(d) for d in range(1, me.F)] + [me.tensor(d) for d in range(1, me.T)]
    greet(peers)
    messages, order, arrival = plan(sizes)
    loads[0].wait()
    features[me.t] = jnp.transpose(inputs_ref[...].astype(jnp.float32)).astype(jnp.bfloat16)
    loads[1].wait()
    all_greeted(peers)

    def copy_of(m, arriving):
        message = messages[m]
        sign = message["sign"]
        shift = sign if arriving else 0
        at, axis = dict(message["at"]), message["axis"]
        rows = pl.ds(*message["rows"])
        if axis in at:
            at[axis] += shift
        if message["part"] == "I":
            core = me.c
            if axis == "c" and arriving:
                core = 1 - me.c
            block = features.at[me.wrap(me.z - at["z"], me.Z) * 2 + core, rows]
            peer = me.sibling() if axis == "c" else me.along_z(sign)
        else:
            y, x = me.wrap(me.y - at["y"], me.Y), me.wrap(me.x - at["x"], me.X)
            block = second.at[y, x, rows] if message["part"] == "A" else first.at[x, y, rows]
            peer = me.plane(0, sign) if axis == "x" else me.plane(sign, 0)
        return remote(block, block, send_sem.at[m], recv_sem.at[m], peer)

    def start_after(event):
        for m in sorted((m for m in range(len(messages)) if messages[m]["needs"] == event), key=lambda m: messages[m]["starts"]):
            copy_of(m, False).start()

    def add(oy, ox):
        y, x = me.wrap(me.y - oy, me.Y), me.wrap(me.x - ox, me.X)
        f = y * me.X + x
        rows = jnp.concatenate([first[x, y], second[y, x]], axis=0)
        columns = pl.ds(pl.multiple_of(lax.rem(f, 2) * 2 * TAPS, 2 * TAPS), 2 * TAPS)
        blended_ref[...] += jnp.dot(features[f // 2, :, columns], rows, preferred_element_type=jnp.float32)

    have = {(part, 0, 0): HALF for part in "AB"}
    ready, pending = [(0, 0)], list(order)
    adding = []

    def features_here():
        return not any(messages[m]["part"] == "I" for m in pending)

    def pump(until):
        while pending and arrival[pending[0]] <= until:
            m = pending.pop(0)
            copy_of(m, True).wait_recv()
            start_after(m)
            message = messages[m]
            if message["part"] != "I":
                at = dict(message["at"])
                at[message["axis"]] += message["sign"]
                place = (at["y"] % me.Y, at["x"] % me.X)
                have[(message["part"],) + place] = have.get((message["part"],) + place, 0) + message["rows"][1]
                if have.get(("A",) + place) == HALF and have.get(("B",) + place) == HALF:
                    ready.append(place)
            for _ in range(2):
                if adding and features_here() and ready:
                    add(*ready.pop(0))

    out = []

    def send(*args):
        out.append(remote(*args))
        out[-1].start()

    def drain():
        for copy in out:
            copy.wait_send()
        out.clear()

    send(grad_ref.at[pl.ds(0, TAPS)], halo, halo_sem.at[0], halo_sem.at[1], me.fsdp(-1))
    start_after("I")
    loads[2].wait()
    strided_taps(filters_ref[...].astype(jnp.float32), toeplitz)
    first[me.x, me.y] = convolve(toeplitz, grad_ref[...])
    start_after("B")
    loads[3].wait()
    basis_terms = in_three(jnp.transpose(basis_ref[...]))

    def times_basis(rows):
        product = 0.0
        for i in range(3):
            term = basis_terms[:, i * rows.shape[1] : (i + 1) * rows.shape[1]]
            product += lax.dot_general(term, rows, (((1,), (1,)), ((), ())), preferred_element_type=jnp.float32)
        return product

    mixed[0] = times_basis(first[me.x, me.y])
    out[0].wait_recv()
    tail = jnp.where(me.f == me.F - 1, jnp.zeros_like(halo[...]), halo[...])
    second[me.y, me.x] = convolve(toeplitz, jnp.concatenate([grad_ref[TAPS:, :], tail], axis=0))
    start_after("A")
    mixed[1] = times_basis(second[me.y, me.x])

    piece = RANK // me.Z
    small = piece // 2

    def core_swap(kind, there, here):
        send(there, here, core_sem.at[kind, 0], core_sem.at[kind, 1], me.sibling())

    def core_here(kind, here):
        remote(here, here, core_sem.at[kind, 0], core_sem.at[kind, 1], me.sibling()).wait_recv()

    def z_scatter(kind, source, into):
        for d in range(1, me.Z):
            send(source.at[me.wrap(me.z + d, me.Z)], into.at[d], z_send.at[kind, d], z_recv.at[kind, d], me.along_z(d))

    def z_collect(kind, source, into):
        total = source[me.z]
        for d in range(1, me.Z):
            remote(into.at[d], into.at[d], z_send.at[kind, d], z_recv.at[kind, d], me.along_z(d)).wait_recv()
            total = total + into[d]
        return total

    def share(part, f):
        rows = part.shape[0] // me.F
        start = f * rows
        return part.at[pl.ds(start if len(part.shape) == 3 else pl.multiple_of(start, 8), rows)]

    def scatter(kind, part, into):
        for d in range(1, me.F):
            send(share(part, me.wrap(me.f + d, me.F)), into.at[d], f_send.at[kind, d], f_recv.at[kind, d], me.fsdp(d))

    def collect(kind, part, into):
        total = share(part, me.f)[...]
        for d in range(1, me.F):
            remote(into.at[d], into.at[d], f_send.at[kind, d], f_recv.at[kind, d], me.fsdp(d)).wait_recv()
            total = total + into[d]
        return total


    def gather_y(kind, block):
        here = block(me.y, me.x)
        for dy in range(1, me.Y):
            send(here, here, p_send.at[kind, 0, dy], p_recv.at[kind, 0, dy], me.plane(dy, 0))
        for dx in range(1, me.X):
            send(here, here, p_send.at[kind, dx, 0], p_recv.at[kind, dx, 0], me.plane(0, dx))

    def gather_x(kind, block):
        for dy in sorted(range(1, me.Y), key=lambda d: min(d, me.Y - d)):
            there = block(me.wrap(me.y - dy, me.Y), me.x)
            remote(there, there, p_send.at[kind, 0, dy], p_recv.at[kind, 0, dy], me.plane(dy, 0)).wait_recv()
            for dx in range(1, me.X):
                send(there, there, p_send.at[kind, dx, dy], p_recv.at[kind, dx, dy], me.plane(0, dx))

    def gathered(kind, block, columns=None):
        for dx in columns or range(1, me.X):
            for dy in range(me.Y):
                there = block(me.wrap(me.y - dy, me.Y), me.wrap(me.x - dx, me.X))
                remote(there, there, p_send.at[kind, dx, dy], p_recv.at[kind, dx, dy], me.plane(0, dx)).wait_recv()

    core_swap(0, mixed.at[1 - me.c], mixed_in)
    loads[4].wait()
    from_momentum = lax.dot_general(
        jnp.transpose(basis_ref[...]), blended_ref[...], (((1,), (1,)), ((), ())),
        precision=HIGHEST, preferred_element_type=jnp.float32,
    )
    for z in range(me.Z):
        for c in range(2):
            at = z * piece + c * small
            partial[c, z] = from_momentum[at : at + small, :]
    core_here(0, mixed_in)
    for z in range(me.Z):
        rows = slice(z * piece, (z + 1) * piece)
        mixed_half[z] = mixed[me.c, rows, :] + mixed_in[rows, :]
    z_scatter(0, mixed_half, mixed_z)
    core_swap(1, partial.at[1 - me.c], half_in)
    pump(WHEN[0])
    core_here(1, half_in)
    half_sum[...] = partial[me.c] + half_in[...]
    pump(WHEN[1])
    mixed_all[me.f] = z_collect(0, mixed_half, mixed_z)

    def mixed_block(y, x):
        return mixed_all.at[y * me.X + x]

    gather_y(0, mixed_block)
    z_scatter(1, half_sum, z_in)
    pump(WHEN[2])
    gather_x(0, mixed_block)
    pump(WHEN[3])
    held = z_collect(1, half_sum, z_in)
    gathered(0, mixed_block)
    while not features_here():
        pump(arrival[pending[0]])

    def add_mixed(pair, total):
        left = jnp.concatenate([mixed_all[2 * pair], mixed_all[2 * pair + 1]], axis=1)
        high = left.astype(jnp.bfloat16)
        rest = left - high.astype(jnp.float32)
        middle = rest.astype(jnp.bfloat16)
        low = (rest - middle.astype(jnp.float32)).astype(jnp.bfloat16)
        columns = [pl.ds(pl.multiple_of(i * 2 * TAPS + me.c * TAPS, TAPS), TAPS) for i in range(2)]
        right = jnp.concatenate([features[pair, :, column] for column in columns], axis=1)
        return total + lax.dot_general(
            jnp.concatenate([high, middle, low], axis=0), right, (((1,), (1,)), ((), ())), preferred_element_type=jnp.float32
        )

    total = lax.fori_loop(0, me.F // 2, add_mixed, jnp.zeros((3 * piece, features.shape[1]), jnp.float32))
    total = total[:piece] + (total[piece : 2 * piece] + total[2 * piece :])
    part[0] = total[:small]
    part[1] = total[small:]
    core_swap(2, part.at[1 - me.c], part_in)
    adding.append(True)
    pump(WHEN[4])
    core_here(2, part_in)
    own = sketch_ref.at[me.c, me.z]
    own[...] = held + (part[me.c] + part_in[...])
    for d in range(1, me.Z):
        send(own, own, z_send.at[2, d], z_recv.at[2, d], me.along_z(d))
    pump(WHEN[5])
    for d in range(1, me.Z):
        there = sketch_ref.at[me.c, me.wrap(me.z - d, me.Z)]
        remote(there, there, z_send.at[2, d], z_recv.at[2, d], me.along_z(d)).wait_recv()
    core_swap(3, sketch_ref.at[me.c], sketch_ref.at[me.c])
    pump(WHEN[6])
    core_here(3, sketch_ref.at[1 - me.c])
    sketch_t = jnp.concatenate([sketch_ref[c, z] for z in range(me.Z) for c in range(2)], axis=0)
    gram = dot_t(sketch_t, sketch_t)
    for c in range(2):
        @pl.when(me.c == c)
        def _():
            for i in range(16):
                for j in range(2):
                    at = 128 * c + 8 * i
                    gram_part[2 * i + j] = gram[at : at + 8, 128 * j : 128 * j + 128]
    scatter(0, gram_part, gram_in)
    sketch = jnp.transpose(sketch_t)
    pump(WHEN[7])
    gram_mine = gram_all.at[me.c]

    def gram_block(y, x):
        return share(gram_mine, y * me.X + x)

    gram_block(me.y, me.x)[...] = collect(0, gram_part, gram_in)
    gather_y(3, gram_block)
    pump(WHEN[8])
    gather_x(3, gram_block)
    pump(1e9)
    while ready:
        add(*ready.pop(0))
    right_part[...] = rows_dot(blended_ref[...], sketch)
    column = right_part.shape[0] // me.X
    block_rows = column // me.Y

    def right_column(x):
        return pl.ds(pl.multiple_of(x * column, 8), column)

    def right_block(y, x):
        return right_ref.at[pl.ds(pl.multiple_of(x * column + y * block_rows, 8), block_rows)]

    for dx in range(1, me.X):
        send(right_part.at[right_column(me.wrap(me.x + dx, me.X))], right_x.at[dx], p_send.at[1, dx, 0], p_recv.at[1, dx, 0], me.plane(0, dx))
    for m in order:
        copy_of(m, False).wait_send()
    gathered(3, gram_block)
    core_swap(4, gram_mine, gram_mine)
    total = right_part[right_column(me.x), :]
    for dx in range(1, me.X):
        remote(right_x.at[dx], right_x.at[dx], p_send.at[1, dx, 0], p_recv.at[1, dx, 0], me.plane(0, dx)).wait_recv()
        total = total + right_x[dx]
    right_mid[...] = total

    def middle_rows(y):
        return pl.ds(pl.multiple_of(y * block_rows, 8), block_rows)

    for dy in range(1, me.Y):
        send(right_mid.at[middle_rows(me.wrap(me.y + dy, me.Y))], right_y.at[dy], p_send.at[1, 0, dy], p_recv.at[1, 0, dy], me.plane(dy, 0))
    core_here(4, gram_all.at[1 - me.c])

    top = jnp.concatenate(inverse_factor([gram_all[0, 2 * i] for i in range(16)]), axis=0)
    total = right_mid[middle_rows(me.y), :]
    for dy in range(1, me.Y):
        remote(right_y.at[dy], right_y.at[dy], p_send.at[1, 0, dy], p_recv.at[1, 0, dy], me.plane(dy, 0)).wait_recv()
        total = total + right_y[dy]
    right_block(me.y, me.x)[...] = total
    gather_y(2, right_block)
    below = jnp.concatenate([gram_all[1, 2 * i] for i in range(16)], axis=0)
    lower = dot_t(below, top)
    rest = jnp.concatenate([gram_all[1, 2 * i + 1] for i in range(16)], axis=0) - dot_t(lower, lower)
    bottom = jnp.concatenate(inverse_factor(by_eight(rest)), axis=0)
    gather_x(2, right_block)
    cross = -dot(bottom, dot(lower, top))
    inverse = jnp.concatenate([
        jnp.concatenate([top, jnp.zeros_like(top)], axis=1), jnp.concatenate([cross, bottom], axis=1)
    ], axis=0)
    orthonormal = dot_t(sketch, inverse)
    orthonormal_ref[...] = orthonormal
    drain()
    total = 0.0
    for dx in sorted(range(me.X), key=lambda d: min(d, me.X - d)):
        if dx:
            gathered(2, right_block, [dx])
        rows = right_column(me.wrap(me.x - dx, me.X))
        projected = dot_t(right_ref[rows, :], inverse)
        projected_ref[rows, :] = projected
        total += jnp.sum(projected * projected, axis=0, keepdims=True)
    squares[0] = total
    for d in range(1, me.T):
        send(squares.at[0], squares.at[d], t_send.at[d], t_recv.at[d], me.tensor(d))
    momentum_ref[...] = blended_ref[...] - (1.0 - momentum_decay) * dot_t(orthonormal, projected_ref[...])
    total = squares[0]
    for d in range(1, me.T):
        remote(squares.at[d], squares.at[d], t_send.at[d], t_recv.at[d], me.tensor(d)).wait_recv()
        total = total + squares[d]
    scale_ref[...] = 1.0 / jnp.sqrt(total / D + epsilon)
    drain()


def finish_kernel(
    orthonormal_ref, projected_ref, momentum_ref, scale_ref, update_hbm, momentum_hbm, basis_hbm, update, basis, sems
):
    out = [pltpu.make_async_copy(momentum_ref, momentum_hbm, sems.at[0])]
    out[0].start()
    basis[...] = projected_ref[...] * scale_ref[...]
    out.append(pltpu.make_async_copy(basis, basis_hbm, sems.at[1]))
    out[1].start()
    update[...] = (math.sqrt(D / RANK) * dot_t(orthonormal_ref[...], basis[...])).astype(jnp.bfloat16)
    out.append(pltpu.make_async_copy(update, update_hbm, sems.at[2]))
    out[2].start()
    for copy in out:
        copy.wait()


def call(kernel, name, outs, scratch, collective, in_space, out_space, *args):
    params = dict(vmem_limit_bytes=56 << 20)
    if collective is not None:
        params.update(collective_id=collective, has_side_effects=True)
    return pl.pallas_call(
        kernel,
        name=name,
        out_shape=[jax.ShapeDtypeStruct(shape, dtype) for shape, dtype in outs],
        in_specs=[in_space] * len(args),
        out_specs=[out_space] * len(outs),
        scratch_shapes=scratch,
        compiler_params=pltpu.CompilerParams(**params),
        cost_estimate=pl.CostEstimate(flops=3 * 10**9, bytes_accessed=4 << 20, transcendentals=0),
    )(*args)


def shards(sizes, inputs, grad_out, filters, momentum, basis):
    X, Y, Z = sizes
    F, T = X * Y, 2 * Z
    dma = pltpu.SemaphoreType.DMA
    f32, bf16 = jnp.float32, jnp.bfloat16
    tokens, channels = grad_out.shape
    width = inputs.shape[1]
    messages, _, _ = plan(sizes)
    orthonormal, projected, momentum, scale = call(
        functools.partial(main_kernel, sizes), "main",
        [((width, RANK), f32), ((channels, RANK), f32), ((width, channels), f32), ((1, RANK), f32)],
        [
            pltpu.VMEM(inputs.shape, bf16), pltpu.VMEM(grad_out.shape, bf16), pltpu.VMEM(filters.shape, bf16),
            pltpu.VMEM(basis.shape, f32), pltpu.VMEM((width, channels), f32),
            pltpu.VMEM((TAPS, channels), bf16),
            pltpu.VMEM((filters.shape[0] * TAPS, 2 * TAPS), bf16),
            pltpu.VMEM((X, Y, HALF, channels), bf16),
            pltpu.VMEM((Y, X, HALF, channels), bf16),
            pltpu.VMEM((T, width, inputs.shape[0]), bf16),
            pltpu.VMEM((2, RANK, TAPS), f32), pltpu.VMEM((RANK, TAPS), f32), pltpu.VMEM((Z, RANK // Z, TAPS), f32),
            pltpu.VMEM((Z, RANK // Z, TAPS), f32), pltpu.VMEM((F, RANK // Z, TAPS), f32),
            pltpu.VMEM((2, Z, RANK // T, width), f32), pltpu.VMEM((Z, RANK // T, width), f32),
            pltpu.VMEM((Z, RANK // T, width), f32), pltpu.VMEM((Z, RANK // T, width), f32),
            pltpu.VMEM((2, RANK // T, width), f32), pltpu.VMEM((RANK // T, width), f32), pltpu.VMEM((2, Z, RANK // T, width), f32),
            pltpu.VMEM((32, 8, 128), f32), pltpu.VMEM((F, 32 // F, 8, 128), f32), pltpu.VMEM((2, 32, 8, 128), f32),
            pltpu.VMEM((channels, RANK), f32), pltpu.VMEM((X, channels // X, RANK), f32), pltpu.VMEM((channels // X, RANK), f32),
            pltpu.VMEM((Y, channels // F, RANK), f32), pltpu.VMEM((channels, RANK), f32),
            pltpu.VMEM((T, 1, RANK), f32),
            dma((5,)), dma((2,)), dma((len(messages),)), dma((len(messages),)), dma((5, 2)),
            dma((3, Z)), dma((3, Z)), dma((1, F)), dma((1, F)), dma((4, X, Y)), dma((4, X, Y)), dma((T,)), dma((T,)),
        ],
        1, ANY, VMEM, inputs, grad_out, filters, momentum, basis,
    )
    return tuple(call(
        finish_kernel, "finish",
        [((width, channels), bf16), ((width, channels), f32), ((channels, RANK), f32)],
        [pltpu.VMEM((width, channels), bf16), pltpu.VMEM((channels, RANK), f32), dma((3,))],
        None, VMEM, ANY, orthonormal, projected, momentum, scale,
    ))


def solution(mesh):
    fsdp, tensor = mesh.shape["fsdp"], mesh.shape["tensor"]
    X = 4 if fsdp == 32 else 2
    placed = (
        P("tensor", "fsdp"),
        P("fsdp", "tensor"),
        P("tensor", None),
        P("fsdp", "tensor"),
        P("tensor", None),
    )
    return jax.shard_map(
        functools.partial(shards, (X, fsdp // X, tensor // 2)),
        mesh=mesh,
        in_specs=placed,
        out_specs=(P("fsdp", "tensor"), P("fsdp", "tensor"), P("tensor", None)),
        check_vma=False,
    )
```
